32 devices in a mesh: grid: 2 (over x), rank: 4 (over y, core), term: 4 (over z).
Axes of the slice: x: 2, y: 2, z: 4, core: 2. Of those that a mesh axis runs over, the one named last changes fastest.
Arguments:
- rhs: float32 [128, 4, 256], P('rank', 'grid')
- coef: float32 [12, 4, 256], P('term', 'grid'), may hold values from 0.03 to 0.3
- env: float32 [12, 128, 128], P('term', 'rank'), as said below
Outputs:
- solution: float32 [128, 4, 256], P('rank', 'grid')
- residual: float32 [128, 4, 256], P('rank', 'grid')
The draws below stay inside these ranges and needn't reach their ends.
Inputs may be any that keep to these rules, and one draw needn't show every extreme that they name: env[k] is a symmetric matrix for every k.
All inputs are finite; a program needn't handle non-finite values.
Results may differ from the reference program's by a relative error of at most 0.0003.
Values sent between devices are 32-bit elements; how exact they have to be, the bound alone decides.
A program may use at most 64 MiB of HBM per device.

```python
import math
import jax
import jax.numpy as jnp
from jax import lax

K = 12
R = 128
NY = 256
ITERS = 4
NX = 4


def draw_rhs(key, part):
    subkeys = jax.random.split(key, 3)
    rank_scale = jnp.exp(jax.random.uniform(subkeys[1], (R, 1, 1), jnp.float32, 0.0, math.log(10.0)))
    x_centre = (jnp.arange(NX, dtype=jnp.float32) + 0.5) / NX
    row_scale = jnp.exp(jax.random.uniform(subkeys[2], (1, NX, 1), jnp.float32, 0.0, math.log(10.0)))
    row_scale = row_scale * (1.0 + 2.0 * x_centre)[None, :, None] / 3.0
    noise = jnp.clip(jax.random.normal(subkeys[0], (R, NX, NY), jnp.float32), -4.0, 4.0)
    return 0.3 * noise * rank_scale * row_scale


def draw_env(key, part):
    subkeys = jax.random.split(jax.random.fold_in(key, 7), 2)
    scatter_part = jax.random.uniform(subkeys[0], (K, R, R), jnp.float32, -1.0 / R, 1.0 / R)
    upper_part = jnp.triu(scatter_part, 1)
    symmetric = upper_part + jnp.swapaxes(upper_part, 1, 2)
    diag_part = 1.0 + jax.random.uniform(subkeys[1], (K, R), jnp.float32, 0.0, 1.0)
    return symmetric + diag_part[:, :, None] * jnp.eye(R, dtype=jnp.float32)[None]


def levels(own_key, dims, cuts, low, high):
    def one(dim, shards_of):
        draws = jax.random.uniform(jax.random.fold_in(jax.random.fold_in(own_key, 6), dim), (shards_of,), jnp.float32, low / len(cuts), high / len(cuts))
        return jnp.repeat(jnp.exp(draws), dims[dim] // shards_of).reshape((-1,) + (1,) * (len(dims) - dim - 1))

    loudness = one(*cuts[0])
    for cut in cuts[1:]:
        loudness = loudness * one(*cut)
    return loudness


def setup_inputs(seed: int = 0) -> dict:
    splits = jax.random.split(jax.random.key(seed), 4)
    rhs = draw_rhs(jax.random.fold_in(splits[3], 71), 0)
    coef = jnp.clip(jnp.exp(math.log(0.3) - 2.3025852 * jax.random.uniform(splits[1], (K, NX, NY), jnp.float32) ** levels(splits[1], (K, NX, NY), ((0, 4), (1, 2)), -0.2, 0.2)), 0.03, 0.3)
    env = draw_env(jax.random.fold_in(splits[3], 71), 0)
    return dict(rhs=rhs, coef=coef, env=env)


def face_weights(padded):
    wide = jnp.pad(padded, ((0, 0), (0, 0), (1, 1)))
    centre = wide[:, 1:-1, 1:-1]
    face_up = 0.5 * (centre + wide[:, 2:, 1:-1])
    face_down = 0.5 * (centre + wide[:, :-2, 1:-1])
    face_right = 0.5 * (centre + wide[:, 1:-1, 2:])
    face_left = 0.5 * (centre + wide[:, 1:-1, :-2])
    return (face_up + face_down + face_right + face_left, face_up, face_down, face_right, face_left)


def apply_faces(field, faces):
    middle = field[..., 1:-1, :]
    sideways = jnp.pad(middle, [(0, 0)] * (middle.ndim - 1) + [(1, 1)])
    total, face_up, face_down, face_right, face_left = faces
    return (total * middle - face_up * field[..., 2:, :] - face_down * field[..., :-2, :]
            - face_right * sideways[..., 2:] - face_left * sideways[..., :-2])


def reference(rhs, coef, env):
    faces = face_weights(jnp.pad(coef, ((0, 0), (1, 1), (0, 0))))

    def operate(field):
        padded = jnp.pad(field, ((0, 0), (1, 1), (0, 0)))
        result = jnp.zeros(field.shape, jnp.float32)
        for term_index in range(K):
            term_faces = tuple(weights[term_index] for weights in faces)
            stenciled = apply_faces(padded, term_faces)
            result = result + jnp.einsum("rs,rxy->sxy", env[term_index], stenciled,
                                         precision=lax.Precision.HIGHEST)
        return result

    solution = jnp.zeros(rhs.shape, jnp.float32)
    residual = rhs
    direction = rhs
    norm_now = jnp.sum(residual * residual)
    for step in range(ITERS):
        image = operate(direction)
        alpha = norm_now / jnp.sum(direction * image)
        solution = solution + alpha * direction
        residual = residual - alpha * image
        norm_next = jnp.sum(residual * residual)
        direction = residual + (norm_next / norm_now) * direction
        norm_now = norm_next
    return solution, residual
```

```python
import functools

import jax
import jax.numpy as jnp
from jax import lax
from jax.experimental import pallas as pl
from jax.experimental.pallas import tpu as pltpu
from jax.sharding import PartitionSpec as P

ITERS = 4
MESH = pl.DeviceIdType.MESH
CHUNK = 16


def padded_2(block, sides, width):
    for axis, dim in sides:
        count = lax.axis_size(axis)
        forward = [(i, i + 1) for i in range(count - 1)]
        backward = [(target, source) for source, target in forward]
        low = lax.ppermute(
            lax.slice_in_dim(block, block.shape[dim] - width, None, axis=dim), axis, forward
        )
        high = lax.ppermute(lax.slice_in_dim(block, 0, width, axis=dim), axis, backward)
        block = jnp.concatenate([low, block, high], axis=dim)
    return block


def face_weights(padded):
    wide = jnp.pad(padded, ((0, 0), (0, 0), (1, 1)))
    centre = wide[:, 1:-1, 1:-1]
    face_up = 0.5 * (centre + wide[:, 2:, 1:-1])
    face_down = 0.5 * (centre + wide[:, :-2, 1:-1])
    face_right = 0.5 * (centre + wide[:, 1:-1, 2:])
    face_left = 0.5 * (centre + wide[:, 1:-1, :-2])
    return (face_up + face_down + face_right + face_left, face_up, face_down, face_right, face_left)


def apply_faces(field, faces):
    middle = field[..., 1:-1, :]
    sideways = jnp.pad(middle, [(0, 0)] * (middle.ndim - 1) + [(1, 1)])
    total, face_up, face_down, face_right, face_left = faces
    return (
        total * middle
        - face_up * field[..., 2:, :]
        - face_down * field[..., :-2, :]
        - face_right * sideways[..., 2:]
        - face_left * sideways[..., :-2]
    )


def shards(rhs, coef, env):
    coef_padded = padded_2(coef, (("grid", 1),), 1)
    faces = tuple((weights[:, None] for weights in face_weights(coef_padded)))

    def square_sum(vector):
        return lax.psum(jnp.sum(vector * vector), ("grid", "rank"))

    solution = jnp.zeros(rhs.shape, jnp.float32)
    residual = rhs
    direction = rhs
    norm_now = square_sum(residual)
    for step in range(ITERS):
        padded = padded_2(direction, (("grid", 1),), 1)
        stenciled = apply_faces(padded[None], faces)
        image = lax.psum_scatter(
            jnp.einsum("krs,krxy->sxy", env, stenciled, precision=lax.Precision.HIGHEST),
            "rank",
            scatter_dimension=0,
            tiled=True,
        )
        image = lax.psum(image, "term")
        alpha = norm_now / lax.psum(jnp.sum(direction * image), ("grid", "rank"))
        solution = solution + alpha * direction
        residual = residual - alpha * image
        norm_next = square_sum(residual)
        direction = residual + norm_next / norm_now * direction
        norm_now = norm_next
    return (solution, residual)


def shift_sum(v):
    lane = lax.broadcasted_iota(jnp.int32, v.shape, v.ndim - 1)
    n = v.shape[-1]
    axis = v.ndim - 1
    left = jnp.where(lane == 0, 0.0, pltpu.roll(v, 1, axis))
    right = jnp.where(lane == n - 1, 0.0, pltpu.roll(v, n - 1, axis))
    return left + right


def neighbours(read, x, count):
    total = shift_sum(read(x))
    if x > 0:
        total = total + read(x - 1)
    if x < count - 1:
        total = total + read(x + 1)
    return total


def split3(v):
    high = v.astype(jnp.bfloat16)
    low = (v - high.astype(jnp.float32)).astype(jnp.bfloat16)
    return jnp.concatenate([high, high, low], axis=0)


def total_sum(v):
    return jnp.sum(v, axis=(0, 1), keepdims=True)


def cg_kernel(
    sizes,
    rhs_ref, coef_ref, env_ref,
    sol_ref, out_ref,
    rhs_own, env_all, coef_all, coef_tab, faces, stack, residual, drive, drive_dir, image_dir, image, keep, down, direction,
    load, rhs_send, rhs_recv, sib_send, sib_recv, env_send, env_recv, envy_send, envy_recv,
    coef_send, coef_recv, img_send, img_recv,
):
    terms, per, rows, strip, ny, ranks = sizes
    grids, ys = 2, 2
    nx = grids * strip
    half = ys * rows
    count = terms * per
    gx = lax.axis_index("grid")
    rank = lax.axis_index("rank")
    gz = lax.axis_index("term")
    gy = rank // 2
    core = rank % 2
    sibling = (gx, gy * 2 + (1 - core), gz)

    def at(x, y, z):
        return (x, y * 2 + core, z)

    origins = [gz + 1 - 2 * (gz % 2), 2 - gz // 2, 3 - 3 * (gz // 2)]
    over_x, over_y, across = at(1 - gx, gy, gz), at(gx, 1 - gy, gz), at(1 - gx, 1 - gy, gz)
    line = [at(gx, gy, o) for o in origins]

    loads = [
        pltpu.make_async_copy(rhs_ref, rhs_own, load.at[0]),
        pltpu.make_async_copy(env_ref, env_all.at[gz, :, gy], load.at[1]),
        pltpu.make_async_copy(coef_ref, coef_all.at[gz, gx], load.at[2]),
    ]
    for copy in loads:
        copy.start()

    barrier = pltpu.get_barrier_semaphore()

    def greet(peer):
        pl.semaphore_signal(barrier, inc=1, device_id=peer, device_id_type=MESH)

    peers = line + [over_x, over_y, across, sibling]
    for peer in peers:
        greet(peer)

    loads[0].wait()
    for i in range(strip):
        residual[gx * strip + i, gy, core] = rhs_own[:, i, :]
    loads[1].wait()
    loads[2].wait()
    pl.semaphore_wait(barrier, len(peers))

    sent = []

    def remote(src, dst, send, recv, device):
        return pltpu.make_async_remote_copy(
            src_ref=src, dst_ref=dst, send_sem=send, recv_sem=recv, device_id=device, device_id_type=MESH
        )

    def push(block, send, recv, device):
        copy = remote(block, block, send, recv, device)
        sent.append(copy)
        copy.start()
        return copy

    def arrived(block, recv):
        remote(block, block, sib_send.at[0], recv, sibling).wait_recv()

    def strip_of(x, y):
        return residual.at[pl.ds(x * strip, strip), y, core]

    def env_line(o):
        return env_all.at[o, :, gy]

    own = strip_of(gx, gy)
    for i in (2, 1, 0):
        push(env_line(gz), env_send.at[i], env_recv.at[gz], line[i])
    rhs_y = push(own, rhs_send.at[0], rhs_recv.at[0], over_y)
    rhs_x = push(own, rhs_send.at[1], rhs_recv.at[1], over_x)
    rhs_d = push(own, rhs_send.at[2], rhs_recv.at[2], across)
    for i in (2, 1, 0):
        push(coef_all.at[gz, gx], coef_send.at[i], coef_recv.at[gz], line[i])
    push(env_line(gz), envy_send.at[3], envy_recv.at[gz], over_y)
    sibs = [push(own, sib_send.at[0], sib_recv.at[0], sibling)]

    def put_stack(o):
        for i in range(per):
            block = env_all[o, i].reshape(half, ranks)
            high = block.astype(jnp.bfloat16)
            low = (block - high.astype(jnp.float32)).astype(jnp.bfloat16)
            for c in range(half // CHUNK):
                at = pl.ds(pl.multiple_of(c * count * CHUNK + (o * per + i) * CHUNK, CHUNK), CHUNK)
                piece = slice(c * CHUNK, (c + 1) * CHUNK)
                stack[at, 0:ranks] = high[piece]
                stack[at, ranks : 2 * ranks] = low[piece]
                stack[at, 2 * ranks : 3 * ranks] = high[piece]

    def cross(i):
        o = origins[i]
        arrived(env_line(o), env_recv.at[o])
        push(env_line(o), envy_send.at[i], envy_recv.at[o], over_y)

    def to_sibling(i, copy, x, y):
        copy.wait_recv()
        sibs.append(push(strip_of(x, y), sib_send.at[i], sib_recv.at[i], sibling))

    def crossed_into_stack(o):
        arrived(env_all.at[o, :, 1 - gy], envy_recv.at[o])
        put_stack(o)

    cross(0)
    to_sibling(1, rhs_y, gx, 1 - gy)
    to_sibling(2, rhs_x, 1 - gx, gy)
    to_sibling(3, rhs_d, 1 - gx, 1 - gy)
    cross(1)
    for o in origins:
        arrived(coef_all.at[o, gx], coef_recv.at[o])
    coef_x = push(coef_all.at[:, gx], coef_send.at[terms - 1], coef_recv.at[gz], over_x)
    cross(2)
    coef_x.wait_recv()
    for x in range(nx):
        for z in range(terms):
            for i in range(per):
                k = z * per + i
                coef_tab[x, k : k + 1, :] = coef_all[z, x // strip, i, x % strip : x % strip + 1, :]
    for x in range(nx):
        here = coef_tab[x]
        lane = lax.broadcasted_iota(jnp.int32, here.shape, 1)
        faces[0, x] = 2.0 * here + 0.5 * neighbours(lambda j: coef_tab[j], x, nx)
        faces[1, x] = jnp.where(lane == ny - 1, 0.0, 0.5 * (here + pltpu.roll(here, ny - 1, 1)))
        faces[2, x] = jnp.where(lane == 0, 0.0, 0.5 * (here + pltpu.roll(here, 1, 1)))
        if x > 0:
            faces[3, x] = 0.5 * (here + coef_tab[x - 1])
        if x < nx - 1:
            faces[4, x] = 0.5 * (here + coef_tab[x + 1])
    for copy in sibs:
        copy.wait_recv()
    for o in [gz] + origins:
        crossed_into_stack(o)
    for copy in sent:
        copy.wait_send()

    def image_copy(x, slot):
        block = image.at[slot, x, :, core]
        return remote(block, block, img_send.at[slot, x], img_recv.at[slot, x], sibling)

    def emit(slot, x, c, value):
        per_y = rows // CHUNK
        image[slot, x, c // per_y, core, (c % per_y) * CHUNK : (c % per_y + 1) * CHUNK, :] = value

    def product(x, field, slot):
        parts = split3(field)
        for c in range(half // CHUNK):
            span = slice(c * count * CHUNK, (c + 1) * count * CHUNK)
            block = jnp.dot(stack[span, :], parts, preferred_element_type=jnp.float32)
            sums = [None] * 5
            for k in range(count):
                term = block[k * CHUNK : (k + 1) * CHUNK]
                for a in range(5):
                    if (a == 3 and x == 0) or (a == 4 and x == nx - 1):
                        continue
                    value = faces[a, x, k : k + 1, :] * term
                    sums[a] = value if sums[a] is None else sums[a] + value
            value = sums[0] - pltpu.roll(sums[1], 1, 1) - pltpu.roll(sums[2], ny - 1, 1)
            piece = slice(c * CHUNK, (c + 1) * CHUNK)
            if x > 0:
                value = value - down[x - 1, piece, :]
                emit(slot, x - 1, c, keep[x - 1, piece, :] - sums[3])
            if x < nx - 1:
                down[x, piece, :] = sums[4]
                keep[x, piece, :] = value
            else:
                emit(slot, x, c, value)
        if x > 0:
            image_copy(x - 1, slot).start()
        if x == nx - 1:
            image_copy(x, slot).start()

    mine = pl.ds(pl.multiple_of(rank * rows, rows), rows)

    def folded(v):
        return jnp.sum(v.reshape(v.shape[0] // 8, 8, v.shape[1]), axis=0)

    square = jnp.zeros((8, ny), jnp.float32)
    for x in range(nx):
        field = residual[x].reshape(ranks, ny)
        square = square + folded(field * field)
        product(x, field, 0)
    norm = total_sum(square)

    alpha = beta = None
    for step in range(ITERS):
        square = jnp.zeros((8, ny), jnp.float32)
        cross_sum = jnp.zeros((8, ny), jnp.float32)
        if step == 1:
            for i in range(strip):
                field = residual[gx * strip + i, gy, core]
                direction[i] = field
                sol_ref[i] = alpha * field
        elif step > 1:
            for i in range(strip):
                field = residual[gx * strip + i, gy, core] + beta * direction[i]
                direction[i] = field
                sol_ref[i] = sol_ref[i] + alpha * field
        for x in range(nx):
            image_copy(x, step).wait_recv()
            for y in range(ys):
                for j in range(2):
                    at = slice((y * 2 + j) * rows, (y * 2 + j + 1) * rows)
                    fresh = image[step, x, y, j]
                    left = residual[x, y, j]
                    if step == 0:
                        now = fresh
                    else:
                        old = drive[x, at, :]
                        if step == 1:
                            first, second = old, fresh
                        else:
                            first = old + beta * image_dir[x, at, :]
                            second = fresh + beta * drive_dir[x, at, :]
                        image_dir[x, at, :] = first
                        if step < ITERS - 1:
                            drive_dir[x, at, :] = second
                        left = left - alpha * first
                        now = old - alpha * second
                        residual[x, y, j] = left
                        square = square + folded(left * left)
                    drive[x, at, :] = now
                    cross_sum = cross_sum + folded(left * now)
            if step < ITERS - 1:
                product(x, drive[x], step + 1)
        slope = total_sum(cross_sum)
        if step == 0:
            alpha = norm / slope
        else:
            fresh_norm = total_sum(square)
            beta = fresh_norm / norm
            alpha = fresh_norm / (slope - beta * fresh_norm / alpha)
            norm = fresh_norm

    for i in range(strip):
        x = gx * strip + i
        left = residual[x, gy, core]
        sol_ref[i] = sol_ref[i] + alpha * (left + beta * direction[i])
        out_ref[i] = left - alpha * (drive[x, mine, :] + beta * image_dir[x, mine, :])
    for slot in range(ITERS):
        for x in range(nx):
            image_copy(x, slot).wait_send()


def fused(mesh, rhs, coef, env):
    terms = mesh.shape["term"]
    rows, strip, ny = rhs.shape
    per, ranks = env.shape[0], env.shape[2]
    grids, ys = 2, 2
    nx, half, count = grids * strip, ys * rows, per * terms
    sizes = (terms, per, rows, strip, ny, ranks)
    f32 = jnp.float32
    dma = pltpu.SemaphoreType.DMA
    block = jax.ShapeDtypeStruct((strip, rows, ny), f32)
    sol, res = pl.pallas_call(
        functools.partial(cg_kernel, sizes),
        out_shape=(block, block),
        in_specs=[pl.BlockSpec(memory_space=pltpu.HBM)] * 3,
        out_specs=(pl.BlockSpec(memory_space=pltpu.VMEM),) * 2,
        scratch_shapes=[
            pltpu.VMEM((rows, strip, ny), f32),
            pltpu.VMEM((terms, per, ys, rows, ranks), f32),
            pltpu.VMEM((terms, grids, per, strip, ny), f32),
            pltpu.VMEM((nx, count, ny), f32),
            pltpu.VMEM((5, nx, count, ny), f32),
            pltpu.VMEM((count * half, 3 * ranks), jnp.bfloat16),
            pltpu.VMEM((nx, ys, 2, rows, ny), f32),
            pltpu.VMEM((nx, ranks, ny), f32),
            pltpu.VMEM((nx, ranks, ny), f32),
            pltpu.VMEM((nx, ranks, ny), f32),
            pltpu.VMEM((ITERS, nx, ys, 2, rows, ny), f32),
            pltpu.VMEM((nx, half, ny), f32),
            pltpu.VMEM((nx, half, ny), f32),
            pltpu.VMEM((strip, rows, ny), f32),
            dma((3,)),
            dma((3,)), dma((3,)),
            dma((4,)), dma((4,)),
            dma((terms - 1,)), dma((terms,)),
            dma((terms,)), dma((terms,)),
            dma((terms,)), dma((terms,)),
            dma((ITERS, nx)), dma((ITERS, nx)),
        ],
        compiler_params=pltpu.CompilerParams(
            collective_id=0, has_side_effects=True, vmem_limit_bytes=63 * 2**20
        ),
    )(rhs, coef, env)
    return sol.transpose(1, 0, 2), res.transpose(1, 0, 2)


def fits(mesh, rhs):
    cells = rhs.shape[1] * mesh.shape["grid"] * rhs.shape[2]
    return mesh.shape["rank"] == 4 and mesh.shape["grid"] == 2 and mesh.shape["term"] == 4 and rhs.shape[0] * 4 * cells * 4 <= 2**20


def solution(mesh):
    placed = (P("rank", "grid", None), P("term", "grid", None), P("term", "rank", None))

    def run(rhs, coef, env):
        if fits(mesh, rhs):
            return fused(mesh, rhs, coef, env)
        return shards(rhs, coef, env)

    return jax.shard_map(
        run,
        mesh=mesh,
        in_specs=placed,
        out_specs=(P("rank", "grid", None), P("rank", "grid", None)),
        check_vma=False,
    )
```

```python
import functools

import jax
import jax.numpy as jnp
from jax import lax
from jax.experimental import pallas as pl
from jax.experimental.pallas import tpu as pltpu
from jax.sharding import PartitionSpec as P

ITERS = 4
MESH = pl.DeviceIdType.MESH
CHUNK = 16


def padded_2(block, sides, width):
    for axis, dim in sides:
        count = lax.axis_size(axis)
        forward = [(i, i + 1) for i in range(count - 1)]
        backward = [(target, source) for source, target in forward]
        low = lax.ppermute(
            lax.slice_in_dim(block, block.shape[dim] - width, None, axis=dim), axis, forward
        )
        high = lax.ppermute(lax.slice_in_dim(block, 0, width, axis=dim), axis, backward)
        block = jnp.concatenate([low, block, high], axis=dim)
    return block


def face_weights(padded):
    wide = jnp.pad(padded, ((0, 0), (0, 0), (1, 1)))
    centre = wide[:, 1:-1, 1:-1]
    face_up = 0.5 * (centre + wide[:, 2:, 1:-1])
    face_down = 0.5 * (centre + wide[:, :-2, 1:-1])
    face_right = 0.5 * (centre + wide[:, 1:-1, 2:])
    face_left = 0.5 * (centre + wide[:, 1:-1, :-2])
    return (face_up + face_down + face_right + face_left, face_up, face_down, face_right, face_left)


def apply_faces(field, faces):
    middle = field[..., 1:-1, :]
    sideways = jnp.pad(middle, [(0, 0)] * (middle.ndim - 1) + [(1, 1)])
    total, face_up, face_down, face_right, face_left = faces
    return (
        total * middle
        - face_up * field[..., 2:, :]
        - face_down * field[..., :-2, :]
        - face_right * sideways[..., 2:]
        - face_left * sideways[..., :-2]
    )


def shards(rhs, coef, env):
    coef_padded = padded_2(coef, (("grid", 1),), 1)
    faces = tuple((weights[:, None] for weights in face_weights(coef_padded)))

    def square_sum(vector):
        return lax.psum(jnp.sum(vector * vector), ("grid", "rank"))

    solution = jnp.zeros(rhs.shape, jnp.float32)
    residual = rhs
    direction = rhs
    norm_now = square_sum(residual)
    for step in range(ITERS):
        padded = padded_2(direction, (("grid", 1),), 1)
        stenciled = apply_faces(padded[None], faces)
        image = lax.psum_scatter(
            jnp.einsum("krs,krxy->sxy", env, stenciled, precision=lax.Precision.HIGHEST),
            "rank",
            scatter_dimension=0,
            tiled=True,
        )
        image = lax.psum(image, "term")
        alpha = norm_now / lax.psum(jnp.sum(direction * image), ("grid", "rank"))
        solution = solution + alpha * direction
        residual = residual - alpha * image
        norm_next = square_sum(residual)
        direction = residual + norm_next / norm_now * direction
        norm_now = norm_next
    return (solution, residual)


def shift_sum(v):
    lane = lax.broadcasted_iota(jnp.int32, v.shape, v.ndim - 1)
    n = v.shape[-1]
    axis = v.ndim - 1
    left = jnp.where(lane == 0, 0.0, pltpu.roll(v, 1, axis))
    right = jnp.where(lane == n - 1, 0.0, pltpu.roll(v, n - 1, axis))
    return left + right


def neighbours(read, x, count):
    total = shift_sum(read(x))
    if x > 0:
        total = total + read(x - 1)
    if x < count - 1:
        total = total + read(x + 1)
    return total


def split3(v):
    high = v.astype(jnp.bfloat16)
    low = (v - high.astype(jnp.float32)).astype(jnp.bfloat16)
    return jnp.concatenate([high, high, low], axis=0)


def total_sum(v):
    return jnp.sum(v, axis=(0, 1), keepdims=True)


def cg_kernel(
    sizes,
    rhs_ref, coef_ref, env_ref,
    sol_ref, out_ref,
    rhs_own, env_all, coef_all, coef_tab, faces, stack, residual, drive, drive_dir, image_dir, image, keep, down, direction, gathered, split_rhs,
    load, rhs_send, rhs_recv, sib_send, sib_recv, env_send, env_recv, envy_send, envy_recv,
    coef_send, coef_recv, img_send, img_recv,
):
    terms, per, rows, strip, ny, ranks = sizes
    grids, ys = 2, 2
    nx = grids * strip
    half = ys * rows
    count = terms * per
    gx = lax.axis_index("grid")
    rank = lax.axis_index("rank")
    gz = lax.axis_index("term")
    gy = rank // 2
    core = rank % 2
    sibling = (gx, gy * 2 + (1 - core), gz)

    def at(x, y, z):
        return (x, y * 2 + core, z)

    origins = [gz + 1 - 2 * (gz % 2), 2 - gz // 2, 3 - 3 * (gz // 2)]
    over_x, over_y, across = at(1 - gx, gy, gz), at(gx, 1 - gy, gz), at(1 - gx, 1 - gy, gz)
    line = [at(gx, gy, o) for o in origins]

    loads = [
        pltpu.make_async_copy(rhs_ref, rhs_own, load.at[0]),
        pltpu.make_async_copy(env_ref, env_all.at[gz, :, gy], load.at[1]),
        pltpu.make_async_copy(coef_ref, coef_all.at[gz, gx], load.at[2]),
    ]
    for copy in loads:
        copy.start()

    barrier = pltpu.get_barrier_semaphore()

    def greet(peer):
        pl.semaphore_signal(barrier, inc=1, device_id=peer, device_id_type=MESH)

    peers = line + [over_x, over_y, across, sibling]
    for peer in peers:
        greet(peer)

    loads[0].wait()
    for i in range(strip):
        residual[gx * strip + i, gy, core] = rhs_own[:, i, :]
    loads[1].wait()
    loads[2].wait()
    pl.semaphore_wait(barrier, len(peers))

    sent = []

    def remote(src, dst, send, recv, device):
        return pltpu.make_async_remote_copy(
            src_ref=src, dst_ref=dst, send_sem=send, recv_sem=recv, device_id=device, device_id_type=MESH
        )

    def push(block, send, recv, device):
        copy = remote(block, block, send, recv, device)
        sent.append(copy)
        copy.start()
        return copy

    def arrived(block, recv):
        remote(block, block, sib_send.at[0], recv, sibling).wait_recv()

    def strip_of(x, y):
        return residual.at[pl.ds(x * strip, strip), y, core]

    def env_line(o):
        return env_all.at[o, :, gy]

    own = strip_of(gx, gy)
    for i in (2, 1, 0):
        push(coef_all.at[gz, gx], coef_send.at[i], coef_recv.at[gz], line[i])
    for i in (2, 1, 0):
        push(env_line(gz), env_send.at[i], env_recv.at[gz], line[i])
    rhs_y = push(own, rhs_send.at[0], rhs_recv.at[0], over_y)
    rhs_x = push(own, rhs_send.at[1], rhs_recv.at[1], over_x)
    rhs_d = push(own, rhs_send.at[2], rhs_recv.at[2], across)
    push(env_line(gz), envy_send.at[3], envy_recv.at[gz], over_y)
    sibs = [push(own, sib_send.at[0], sib_recv.at[0], sibling)]

    def put_stack(o):
        for i in range(per):
            block = env_all[o, i].reshape(half, ranks)
            high = block.astype(jnp.bfloat16)
            low = (block - high.astype(jnp.float32)).astype(jnp.bfloat16)
            for c in range(half // CHUNK):
                at = pl.ds(pl.multiple_of(c * count * CHUNK + (o * per + i) * CHUNK, CHUNK), CHUNK)
                piece = slice(c * CHUNK, (c + 1) * CHUNK)
                stack[at, 0:ranks] = high[piece]
                stack[at, ranks : 2 * ranks] = low[piece]
                stack[at, 2 * ranks : 3 * ranks] = high[piece]

    def cross(i):
        o = origins[i]
        arrived(env_line(o), env_recv.at[o])
        push(env_line(o), envy_send.at[i], envy_recv.at[o], over_y)

    def to_sibling(i, copy, x, y):
        copy.wait_recv()
        sibs.append(push(strip_of(x, y), sib_send.at[i], sib_recv.at[i], sibling))

    def crossed_into_stack(o):
        arrived(env_all.at[o, :, 1 - gy], envy_recv.at[o])
        put_stack(o)

    for o in origins:
        arrived(coef_all.at[o, gx], coef_recv.at[o])
    coef_x = push(coef_all.at[:, gx], coef_send.at[terms - 1], coef_recv.at[gz], over_x)
    cross(0)
    to_sibling(1, rhs_y, gx, 1 - gy)
    to_sibling(2, rhs_x, 1 - gx, gy)
    cross(1)
    to_sibling(3, rhs_d, 1 - gx, 1 - gy)
    cross(2)
    coef_x.wait_recv()
    for x in range(nx):
        for i in range(per):
            coef_tab[x, :, i, :] = coef_all[:, x // strip, i, x % strip, :]
    for x in range(nx):
        here = coef_tab[x]
        lane = lax.broadcasted_iota(jnp.int32, here.shape, 2)
        faces[0, x] = 2.0 * here + 0.5 * neighbours(lambda j: coef_tab[j], x, nx)
        faces[1, x] = jnp.where(lane == ny - 1, 0.0, 0.5 * (here + pltpu.roll(here, ny - 1, 2)))
        faces[2, x] = jnp.where(lane == 0, 0.0, 0.5 * (here + pltpu.roll(here, 1, 2)))
        if x > 0:
            faces[3, x] = 0.5 * (here + coef_tab[x - 1])
        if x < nx - 1:
            faces[4, x] = 0.5 * (here + coef_tab[x + 1])

    def image_copy(x, slot):
        block = image.at[slot, x, :, core]
        return remote(block, block, img_send.at[slot, x], img_recv.at[slot, x], sibling)

    def emit(slot, x, c, value):
        per_y = rows // CHUNK
        image[slot, x, c // per_y, core, (c % per_y) * CHUNK : (c % per_y + 1) * CHUNK, :] = value

    def weighted(block, x, pairs, sums):
        for n, (z, i) in enumerate(pairs):
            term = block[n * CHUNK : (n + 1) * CHUNK]
            for a in range(5):
                if (a == 3 and x == 0) or (a == 4 and x == nx - 1):
                    continue
                value = faces[a, x, z, i : i + 1, :] * term
                sums[a] = value if sums[a] is None else sums[a] + value

    def settle(x, c, slot, sums):
        value = sums[0] - pltpu.roll(sums[1], 1, 1) - pltpu.roll(sums[2], ny - 1, 1)
        piece = slice(c * CHUNK, (c + 1) * CHUNK)
        if x > 0:
            value = value - down[x - 1, piece, :]
            emit(slot, x - 1, c, keep[x - 1, piece, :] - sums[3])
        if x < nx - 1:
            down[x, piece, :] = sums[4]
            keep[x, piece, :] = value
        else:
            emit(slot, x, c, value)

    def send_rows(x, slot):
        if x > 0:
            image_copy(x - 1, slot).start()
        if x == nx - 1:
            image_copy(x, slot).start()

    def product(x, field, slot):
        parts = split3(field)
        for c in range(half // CHUNK):
            span = slice(c * count * CHUNK, (c + 1) * count * CHUNK)
            block = jnp.dot(stack[span, :], parts, preferred_element_type=jnp.float32)
            sums = [None] * 5
            weighted(block, x, [(z, i) for z in range(terms) for i in range(per)], sums)
            settle(x, c, slot, sums)
        send_rows(x, slot)

    def first_product(o, begin, end):
        wide = per * CHUNK
        for x in range(nx):
            lines = [
                stack[pl.ds(pl.multiple_of((c * terms + o) * wide, CHUNK), wide), :]
                for c in range(half // CHUNK)
            ]
            block = jnp.dot(jnp.concatenate(lines, axis=0), split_rhs[x], preferred_element_type=jnp.float32)
            for c in range(half // CHUNK):
                piece = slice(c * CHUNK, (c + 1) * CHUNK)
                used = [a for a in range(5) if not ((a == 3 and x == 0) or (a == 4 and x == nx - 1))]
                sums = [None] * 5
                if not begin:
                    for a in used:
                        sums[a] = gathered[a, x, piece, :]
                weighted(block[c * wide : (c + 1) * wide], x, [(o, i) for i in range(per)], sums)
                if end:
                    settle(x, c, 0, sums)
                else:
                    for a in used:
                        gathered[a, x, piece, :] = sums[a]
            if end:
                send_rows(x, 0)

    mine = pl.ds(pl.multiple_of(rank * rows, rows), rows)

    def folded(v):
        return jnp.sum(v.reshape(v.shape[0] // 8, 8, v.shape[1]), axis=0)

    crossed_into_stack(gz)
    for copy in sibs:
        copy.wait_recv()
    square = jnp.zeros((8, ny), jnp.float32)
    for x in range(nx):
        field = residual[x].reshape(ranks, ny)
        square = square + folded(field * field)
        split_rhs[x] = split3(field)
    norm = total_sum(square)
    first_product(gz, True, False)
    for i, o in enumerate(origins):
        crossed_into_stack(o)
        first_product(o, False, i == len(origins) - 1)
    for copy in sent:
        copy.wait_send()

    alpha = beta = None
    for step in range(ITERS):
        square = jnp.zeros((8, ny), jnp.float32)
        cross_sum = jnp.zeros((8, ny), jnp.float32)
        if step == 1:
            for i in range(strip):
                field = residual[gx * strip + i, gy, core]
                direction[i] = field
                sol_ref[i] = alpha * field
        elif step > 1:
            for i in range(strip):
                field = residual[gx * strip + i, gy, core] + beta * direction[i]
                direction[i] = field
                sol_ref[i] = sol_ref[i] + alpha * field
        for x in range(nx):
            image_copy(x, step).wait_recv()
            for y in range(ys):
                for j in range(2):
                    at = slice((y * 2 + j) * rows, (y * 2 + j + 1) * rows)
                    fresh = image[step, x, y, j]
                    left = residual[x, y, j]
                    if step == 0:
                        now = fresh
                    else:
                        old = drive[x, at, :]
                        if step == 1:
                            first, second = old, fresh
                        else:
                            first = old + beta * image_dir[x, at, :]
                            second = fresh + beta * drive_dir[x, at, :]
                        image_dir[x, at, :] = first
                        if step < ITERS - 1:
                            drive_dir[x, at, :] = second
                        left = left - alpha * first
                        now = old - alpha * second
                        residual[x, y, j] = left
                        square = square + folded(left * left)
                    drive[x, at, :] = now
                    cross_sum = cross_sum + folded(left * now)
            if step < ITERS - 1:
                product(x, drive[x], step + 1)
        slope = total_sum(cross_sum)
        if step == 0:
            alpha = norm / slope
        else:
            fresh_norm = total_sum(square)
            beta = fresh_norm / norm
            alpha = fresh_norm / (slope - beta * fresh_norm / alpha)
            norm = fresh_norm

    for i in range(strip):
        x = gx * strip + i
        left = residual[x, gy, core]
        sol_ref[i] = sol_ref[i] + alpha * (left + beta * direction[i])
        out_ref[i] = left - alpha * (drive[x, mine, :] + beta * image_dir[x, mine, :])
    for slot in range(ITERS):
        for x in range(nx):
            image_copy(x, slot).wait_send()


def fused(mesh, rhs, coef, env):
    terms = mesh.shape["term"]
    rows, strip, ny = rhs.shape
    per, ranks = env.shape[0], env.shape[2]
    grids, ys = 2, 2
    nx, half, count = grids * strip, ys * rows, per * terms
    sizes = (terms, per, rows, strip, ny, ranks)
    f32 = jnp.float32
    dma = pltpu.SemaphoreType.DMA
    block = jax.ShapeDtypeStruct((strip, rows, ny), f32)
    sol, res = pl.pallas_call(
        functools.partial(cg_kernel, sizes),
        out_shape=(block, block),
        in_specs=[pl.BlockSpec(memory_space=pltpu.HBM)] * 3,
        out_specs=(pl.BlockSpec(memory_space=pltpu.VMEM),) * 2,
        scratch_shapes=[
            pltpu.VMEM((rows, strip, ny), f32),
            pltpu.VMEM((terms, per, ys, rows, ranks), f32),
            pltpu.VMEM((terms, grids, per, strip, ny), f32),
            pltpu.VMEM((nx, terms, per, ny), f32),
            pltpu.VMEM((5, nx, terms, per, ny), f32),
            pltpu.VMEM((count * half, 3 * ranks), jnp.bfloat16),
            pltpu.VMEM((nx, ys, 2, rows, ny), f32),
            pltpu.VMEM((nx, ranks, ny), f32),
            pltpu.VMEM((nx, ranks, ny), f32),
            pltpu.VMEM((nx, ranks, ny), f32),
            pltpu.VMEM((ITERS, nx, ys, 2, rows, ny), f32),
            pltpu.VMEM((nx, half, ny), f32),
            pltpu.VMEM((nx, half, ny), f32),
            pltpu.VMEM((strip, rows, ny), f32),
            pltpu.VMEM((5, nx, half, ny), f32),
            pltpu.VMEM((nx, 3 * ranks, ny), jnp.bfloat16),
            dma((3,)),
            dma((3,)), dma((3,)),
            dma((4,)), dma((4,)),
            dma((terms - 1,)), dma((terms,)),
            dma((terms,)), dma((terms,)),
            dma((terms,)), dma((terms,)),
            dma((ITERS, nx)), dma((ITERS, nx)),
        ],
        compiler_params=pltpu.CompilerParams(
            collective_id=0, has_side_effects=True, vmem_limit_bytes=63 * 2**20
        ),
    )(rhs, coef, env)
    def place(a_ref, b_ref, c_ref, d_ref):
        for i in range(strip):
            c_ref[:, i, :] = a_ref[i]
            d_ref[:, i, :] = b_ref[i]

    final = jax.ShapeDtypeStruct((rows, strip, ny), f32)
    return pl.pallas_call(
        place,
        out_shape=(final, final),
        in_specs=[pl.BlockSpec(memory_space=pltpu.VMEM)] * 2,
        out_specs=(pl.BlockSpec(memory_space=pltpu.VMEM),) * 2,
    )(sol, res)


def fits(mesh, rhs):
    cells = rhs.shape[1] * mesh.shape["grid"] * rhs.shape[2]
    return mesh.shape["rank"] == 4 and mesh.shape["grid"] == 2 and mesh.shape["term"] == 4 and rhs.shape[0] * 4 * cells * 4 <= 2**20


def solution(mesh):
    placed = (P("rank", "grid", None), P("term", "grid", None), P("term", "rank", None))

    def run(rhs, coef, env):
        if fits(mesh, rhs):
            return fused(mesh, rhs, coef, env)
        return shards(rhs, coef, env)

    return jax.shard_map(
        run,
        mesh=mesh,
        in_specs=placed,
        out_specs=(P("rank", "grid", None), P("rank", "grid", None)),
        check_vma=False,
    )
```

```python
import functools

import jax
import jax.numpy as jnp
from jax import lax
from jax.experimental import pallas as pl
from jax.experimental.pallas import tpu as pltpu
from jax.sharding import PartitionSpec as P

ITERS = 4
MESH = pl.DeviceIdType.MESH
CHUNK = 16


def padded_2(block, sides, width):
    for axis, dim in sides:
        count = lax.axis_size(axis)
        forward = [(i, i + 1) for i in range(count - 1)]
        backward = [(target, source) for source, target in forward]
        low = lax.ppermute(
            lax.slice_in_dim(block, block.shape[dim] - width, None, axis=dim), axis, forward
        )
        high = lax.ppermute(lax.slice_in_dim(block, 0, width, axis=dim), axis, backward)
        block = jnp.concatenate([low, block, high], axis=dim)
    return block


def face_weights(padded):
    wide = jnp.pad(padded, ((0, 0), (0, 0), (1, 1)))
    centre = wide[:, 1:-1, 1:-1]
    face_up = 0.5 * (centre + wide[:, 2:, 1:-1])
    face_down = 0.5 * (centre + wide[:, :-2, 1:-1])
    face_right = 0.5 * (centre + wide[:, 1:-1, 2:])
    face_left = 0.5 * (centre + wide[:, 1:-1, :-2])
    return (face_up + face_down + face_right + face_left, face_up, face_down, face_right, face_left)


def apply_faces(field, faces):
    middle = field[..., 1:-1, :]
    sideways = jnp.pad(middle, [(0, 0)] * (middle.ndim - 1) + [(1, 1)])
    total, face_up, face_down, face_right, face_left = faces
    return (
        total * middle
        - face_up * field[..., 2:, :]
        - face_down * field[..., :-2, :]
        - face_right * sideways[..., 2:]
        - face_left * sideways[..., :-2]
    )


def shards(rhs, coef, env):
    coef_padded = padded_2(coef, (("grid", 1),), 1)
    faces = tuple((weights[:, None] for weights in face_weights(coef_padded)))

    def square_sum(vector):
        return lax.psum(jnp.sum(vector * vector), ("grid", "rank"))

    solution = jnp.zeros(rhs.shape, jnp.float32)
    residual = rhs
    direction = rhs
    norm_now = square_sum(residual)
    for step in range(ITERS):
        padded = padded_2(direction, (("grid", 1),), 1)
        stenciled = apply_faces(padded[None], faces)
        image = lax.psum_scatter(
            jnp.einsum("krs,krxy->sxy", env, stenciled, precision=lax.Precision.HIGHEST),
            "rank",
            scatter_dimension=0,
            tiled=True,
        )
        image = lax.psum(image, "term")
        alpha = norm_now / lax.psum(jnp.sum(direction * image), ("grid", "rank"))
        solution = solution + alpha * direction
        residual = residual - alpha * image
        norm_next = square_sum(residual)
        direction = residual + norm_next / norm_now * direction
        norm_now = norm_next
    return (solution, residual)


def shift_sum(v):
    lane = lax.broadcasted_iota(jnp.int32, v.shape, v.ndim - 1)
    n = v.shape[-1]
    axis = v.ndim - 1
    left = jnp.where(lane == 0, 0.0, pltpu.roll(v, 1, axis))
    right = jnp.where(lane == n - 1, 0.0, pltpu.roll(v, n - 1, axis))
    return left + right


def neighbours(read, x, count):
    total = shift_sum(read(x))
    if x > 0:
        total = total + read(x - 1)
    if x < count - 1:
        total = total + read(x + 1)
    return total


def split3(v):
    high = v.astype(jnp.bfloat16)
    low = (v - high.astype(jnp.float32)).astype(jnp.bfloat16)
    return jnp.concatenate([high, high, low], axis=0)


def total_sum(v):
    return jnp.sum(v, axis=(0, 1), keepdims=True)


def cg_kernel(
    sizes,
    rhs_ref, coef_ref, env_ref,
    sol_ref, out_ref,
    rhs_own, env_all, coef_all, coef_tab, faces, stack, residual, image, keep, down, gathered, split_rhs, trace, gram,
    load, rhs_send, rhs_recv, sib_send, sib_recv, env_send, env_recv, envy_send, envy_recv,
    coef_send, coef_recv, img_send, img_recv, sum_send, sum_recv,
):
    terms, per, rows, strip, ny, ranks = sizes
    grids, ys = 2, 2
    nx = grids * strip
    half = ys * rows
    count = terms * per
    gx = lax.axis_index("grid")
    rank = lax.axis_index("rank")
    gz = lax.axis_index("term")
    gy = rank // 2
    core = rank % 2
    sibling = (gx, gy * 2 + (1 - core), gz)

    def at(x, y, z):
        return (x, y * 2 + core, z)

    origins = [gz + 1 - 2 * (gz % 2), 2 - gz // 2, 3 - 3 * (gz // 2)]
    over_x, over_y, across = at(1 - gx, gy, gz), at(gx, 1 - gy, gz), at(1 - gx, 1 - gy, gz)
    line = [at(gx, gy, o) for o in origins]

    loads = [
        pltpu.make_async_copy(rhs_ref, rhs_own, load.at[0]),
        pltpu.make_async_copy(env_ref, env_all.at[gz, :, gy], load.at[1]),
        pltpu.make_async_copy(coef_ref, coef_all.at[gz, gx], load.at[2]),
    ]
    for copy in loads:
        copy.start()

    barrier = pltpu.get_barrier_semaphore()

    def greet(peer):
        pl.semaphore_signal(barrier, inc=1, device_id=peer, device_id_type=MESH)

    peers = line + [over_x, over_y, across, sibling]
    for peer in peers:
        greet(peer)

    loads[0].wait()
    for i in range(strip):
        residual[gx * strip + i, gy, core] = rhs_own[:, i, :]
    loads[1].wait()
    loads[2].wait()
    pl.semaphore_wait(barrier, len(peers))

    sent = []

    def remote(src, dst, send, recv, device):
        return pltpu.make_async_remote_copy(
            src_ref=src, dst_ref=dst, send_sem=send, recv_sem=recv, device_id=device, device_id_type=MESH
        )

    def push(block, send, recv, device):
        copy = remote(block, block, send, recv, device)
        sent.append(copy)
        copy.start()
        return copy

    def arrived(block, recv):
        remote(block, block, sib_send.at[0], recv, sibling).wait_recv()

    def strip_of(x, y):
        return residual.at[pl.ds(x * strip, strip), y, core]

    def env_line(o):
        return env_all.at[o, :, gy]

    own = strip_of(gx, gy)
    for i in (2, 1, 0):
        push(coef_all.at[gz, gx], coef_send.at[i], coef_recv.at[gz], line[i])
    for i in (2, 1, 0):
        push(env_line(gz), env_send.at[i], env_recv.at[gz], line[i])
    rhs_y = push(own, rhs_send.at[0], rhs_recv.at[0], over_y)
    rhs_x = push(own, rhs_send.at[1], rhs_recv.at[1], over_x)
    rhs_d = push(own, rhs_send.at[2], rhs_recv.at[2], across)
    push(env_line(gz), envy_send.at[3], envy_recv.at[gz], over_y)
    sibs = [push(own, sib_send.at[0], sib_recv.at[0], sibling)]

    def put_stack(o):
        for i in range(per):
            block = env_all[o, i].reshape(half, ranks)
            high = block.astype(jnp.bfloat16)
            low = (block - high.astype(jnp.float32)).astype(jnp.bfloat16)
            for c in range(half // CHUNK):
                at = pl.ds(pl.multiple_of(c * count * CHUNK + (o * per + i) * CHUNK, CHUNK), CHUNK)
                piece = slice(c * CHUNK, (c + 1) * CHUNK)
                stack[at, 0:ranks] = high[piece]
                stack[at, ranks : 2 * ranks] = low[piece]
                stack[at, 2 * ranks : 3 * ranks] = high[piece]

    def cross(i):
        o = origins[i]
        arrived(env_line(o), env_recv.at[o])
        push(env_line(o), envy_send.at[i], envy_recv.at[o], over_y)

    def to_sibling(i, copy, x, y):
        copy.wait_recv()
        sibs.append(push(strip_of(x, y), sib_send.at[i], sib_recv.at[i], sibling))

    def crossed_into_stack(o):
        arrived(env_all.at[o, :, 1 - gy], envy_recv.at[o])
        put_stack(o)

    for o in origins:
        arrived(coef_all.at[o, gx], coef_recv.at[o])
    coef_x = push(coef_all.at[:, gx], coef_send.at[terms - 1], coef_recv.at[gz], over_x)
    cross(0)
    to_sibling(1, rhs_y, gx, 1 - gy)
    to_sibling(2, rhs_x, 1 - gx, gy)
    cross(1)
    to_sibling(3, rhs_d, 1 - gx, 1 - gy)
    cross(2)
    coef_x.wait_recv()
    for x in range(nx):
        for i in range(per):
            coef_tab[x, :, i, :] = coef_all[:, x // strip, i, x % strip, :]
    for x in range(nx):
        here = coef_tab[x]
        lane = lax.broadcasted_iota(jnp.int32, here.shape, 2)
        faces[0, x] = 2.0 * here + 0.5 * neighbours(lambda j: coef_tab[j], x, nx)
        faces[1, x] = jnp.where(lane == ny - 1, 0.0, 0.5 * (here + pltpu.roll(here, ny - 1, 2)))
        faces[2, x] = jnp.where(lane == 0, 0.0, 0.5 * (here + pltpu.roll(here, 1, 2)))
        if x > 0:
            faces[3, x] = 0.5 * (here + coef_tab[x - 1])
        if x < nx - 1:
            faces[4, x] = 0.5 * (here + coef_tab[x + 1])

    def image_copy(x, slot):
        block = image.at[slot, pl.ds(x, 2 if x == nx - 2 else 1), :, core]
        return remote(block, block, img_send.at[slot, x], img_recv.at[slot, x], sibling)

    per_y = rows // CHUNK

    def vector(t, x, y, span=slice(None)):
        ref = residual if t == 0 else image.at[t - 1]
        return ref[x, y, core, span, :]

    def emit(slot, x, c, value):
        span = slice((c % per_y) * CHUNK, (c % per_y + 1) * CHUNK)
        image[slot, x, c // per_y, core, span, :] = value * inverse - vector(slot, x, c // per_y, span)

    def weighted(block, x, pairs, sums):
        for n, (z, i) in enumerate(pairs):
            term = block[n * CHUNK : (n + 1) * CHUNK]
            for a in range(5):
                if (a == 3 and x == 0) or (a == 4 and x == nx - 1):
                    continue
                value = faces[a, x, z, i : i + 1, :] * term
                sums[a] = value if sums[a] is None else sums[a] + value

    def settle(x, c, slot, sums):
        value = sums[0] - pltpu.roll(sums[1], 1, 1) - pltpu.roll(sums[2], ny - 1, 1)
        piece = slice(c * CHUNK, (c + 1) * CHUNK)
        if x > 0:
            value = value - down[x - 1, piece, :]
            emit(slot, x - 1, c, keep[x - 1, piece, :] - sums[3])
        if x < nx - 1:
            down[x, piece, :] = sums[4]
            keep[x, piece, :] = value
        else:
            emit(slot, x, c, value)

    def send_rows(x, slot):
        if slot < ITERS - 1 and x > 0 and x < nx - 1:
            image_copy(x - 1, slot).start()
        elif slot < ITERS - 1 and x == nx - 1:
            image_copy(nx - 2, slot).start()

    def product(x, field, slot):
        parts = split3(field)
        for c in range(half // CHUNK):
            span = slice(c * count * CHUNK, (c + 1) * count * CHUNK)
            block = jnp.dot(stack[span, :], parts, preferred_element_type=jnp.float32)
            sums = [None] * 5
            weighted(block, x, [(z, i) for z in range(terms) for i in range(per)], sums)
            settle(x, c, slot, sums)
        send_rows(x, slot)

    def first_product(o, begin, end):
        wide = per * CHUNK
        for x in range(nx):
            lines = [
                stack[pl.ds(pl.multiple_of((c * terms + o) * wide, CHUNK), wide), :]
                for c in range(half // CHUNK)
            ]
            block = jnp.dot(jnp.concatenate(lines, axis=0), split_rhs[x], preferred_element_type=jnp.float32)
            for c in range(half // CHUNK):
                piece = slice(c * CHUNK, (c + 1) * CHUNK)
                used = [a for a in range(5) if not ((a == 3 and x == 0) or (a == 4 and x == nx - 1))]
                sums = [None] * 5
                if not begin:
                    for a in used:
                        sums[a] = gathered[a, x, piece, :]
                weighted(block[c * wide : (c + 1) * wide], x, [(o, i) for i in range(per)], sums)
                if end:
                    settle(x, c, 0, sums)
                else:
                    for a in used:
                        gathered[a, x, piece, :] = sums[a]
            if end:
                send_rows(x, 0)

    def folded(v):
        return jnp.sum(v.reshape(v.shape[0] // 8, 8, v.shape[1]), axis=0)

    def paired(block, send):
        return remote(block, block, sum_send.at[send], sum_recv.at[send], sibling)

    def diagonal():
        shape = (rows, ranks)
        row = lax.broadcasted_iota(jnp.int32, shape, 0)
        column = lax.broadcasted_iota(jnp.int32, shape, 1)
        on = column == row + rank * rows
        weight = faces[0, 0]
        for x in range(1, nx):
            weight = weight + faces[0, x]
        weight = jnp.sum(weight, axis=2, keepdims=True)
        total = jnp.zeros((8, ranks), jnp.float32)
        for z in range(terms):
            for i in range(per):
                entries = jnp.where(on, jnp.abs(env_all[z, i, gy]), 0.0)
                total = total + weight[z, i : i + 1, :] * folded(entries)
        return total

    def grams(part, pairs):
        sums = [None] * len(pairs)
        needed = sorted({t for pair in pairs for t in pair})
        for x in range(nx):
            for y in range(ys):
                fields = {t: vector(t, x, y) for t in needed}
                for n, (i, j) in enumerate(pairs):
                    value = folded(fields[i] * fields[j])
                    sums[n] = value if sums[n] is None else sums[n] + value
        for value, pair in zip(sums, pairs):
            line = jnp.sum(sum(value[:, l : l + 128] for l in range(0, ny, 128)), axis=0, keepdims=True)
            n = order[part].index(pair)
            gram[part, core, n : n + 1, :] = line

    def gram_copy(part):
        return paired(gram.at[part, core], part)

    def gram_sums(part):
        both = jnp.sum(gram[part, 0] + gram[part, 1], axis=1, keepdims=True)
        return {pair: both[n : n + 1, :] for n, pair in enumerate(order[part])}

    last = ITERS
    order = (
        [(i, j) for j in range(last) for i in range(j + 1)],
        [(i, last) for i in range(last)],
    )

    crossed_into_stack(gz)
    for copy in sibs:
        copy.wait_recv()
    for x in range(nx):
        split_rhs[x] = split3(residual[x].reshape(ranks, ny))
    trace[core] = diagonal()
    trace_copy = paired(trace.at[core], 2)
    trace_copy.start()
    gram[...] = jnp.zeros_like(gram)
    inverse = None
    first_product(gz, True, False)
    for i, o in enumerate(origins):
        crossed_into_stack(o)
        if i == len(origins) - 1:
            trace_copy.wait_recv()
            size = total_sum(trace[0] + trace[1]) * (1.0 / (half * nx * ny))
            theta = jnp.where(size > 0.0, size, 1.0)
            inverse = 1.0 / theta
        first_product(o, False, i == len(origins) - 1)
    grams(0, [(0, 0), (0, 1), (1, 1)])

    def mixed(left, right, table):
        total = None
        for i, a in enumerate(left):
            inner = None
            for j, b in enumerate(right):
                value = b * table[min(i, j), max(i, j)]
                inner = value if inner is None else inner + value
            total = a * inner if total is None else total + a * inner
        return total

    def applied(d):
        return [d[0]] + [d[j] + d[j - 1] for j in range(1, len(d))] + [d[-1]]

    def updated(sol, left, d, image_d, alpha):
        sol = [a + alpha * b for a, b in zip(sol, d)] + [alpha * b for b in d[len(sol) :]]
        left = [a - alpha * b for a, b in zip(left, image_d)] + [-alpha * image_d[-1]]
        return sol, left

    for step in range(1, ITERS):
        for x in range(nx):
            if x < nx - 1:
                image_copy(x, step - 1).wait_recv()
            if step == ITERS - 1 and x == nx - 1:
                gram_copy(0).wait_recv()
            product(x, image[step - 1, x].reshape(ranks, ny), step)
        if step < ITERS - 1:
            grams(0, [(i, step + 1) for i in range(step + 2)])
            if step == ITERS - 2:
                gram_copy(0).start()

    table = gram_sums(0)
    one = jnp.ones_like(theta)
    sol, left, d, norm = [], [one], [one], table[0, 0]
    for step in range(ITERS - 1):
        image_d = applied(d)
        alpha = norm / mixed(d, image_d, table)
        sol, left = updated(sol, left, d, image_d, alpha)
        fresh = mixed(left, left, table)
        beta = fresh / norm
        d = [a + beta * b for a, b in zip(left, d)] + [left[-1]]
        norm = fresh
    image_d = applied(d)
    known = mixed(d, image_d[:-1], table)

    grams(1, order[1])
    copy = gram_copy(1)
    copy.start()
    copy.wait_recv()
    rest = gram_sums(1)
    tail = sum(d[i] * rest[i, last] for i in range(last))
    alpha = norm / (known + image_d[-1] * tail)
    sol, left = updated(sol, left, d, image_d, alpha)
    sol = [a * inverse for a in sol]
    for i in range(strip):
        fields = [vector(t, gx * strip + i, gy) for t in range(ITERS + 1)]
        sol_ref[i] = sum(a * v for a, v in zip(sol, fields))
        out_ref[i] = sum(a * v for a, v in zip(left, fields))

    for slot in range(ITERS - 1):
        for x in range(nx - 1):
            image_copy(x, slot).wait_send()
    for copy in sent + [trace_copy, gram_copy(0), gram_copy(1)]:
        copy.wait_send()


def fused(mesh, rhs, coef, env):
    terms = mesh.shape["term"]
    rows, strip, ny = rhs.shape
    per, ranks = env.shape[0], env.shape[2]
    grids, ys = 2, 2
    nx, half, count = grids * strip, ys * rows, per * terms
    sizes = (terms, per, rows, strip, ny, ranks)
    f32 = jnp.float32
    dma = pltpu.SemaphoreType.DMA
    block = jax.ShapeDtypeStruct((strip, rows, ny), f32)
    sol, res = pl.pallas_call(
        functools.partial(cg_kernel, sizes),
        out_shape=(block, block),
        in_specs=[pl.BlockSpec(memory_space=pltpu.HBM)] * 3,
        out_specs=(pl.BlockSpec(memory_space=pltpu.VMEM),) * 2,
        scratch_shapes=[
            pltpu.VMEM((rows, strip, ny), f32),
            pltpu.VMEM((terms, per, ys, rows, ranks), f32),
            pltpu.VMEM((terms, grids, per, strip, ny), f32),
            pltpu.VMEM((nx, terms, per, ny), f32),
            pltpu.VMEM((5, nx, terms, per, ny), f32),
            pltpu.VMEM((count * half, 3 * ranks), jnp.bfloat16),
            pltpu.VMEM((nx, ys, 2, rows, ny), f32),
            pltpu.VMEM((ITERS, nx, ys, 2, rows, ny), f32),
            pltpu.VMEM((nx, half, ny), f32),
            pltpu.VMEM((nx, half, ny), f32),
            pltpu.VMEM((5, nx, half, ny), f32),
            pltpu.VMEM((nx, 3 * ranks, ny), jnp.bfloat16),
            pltpu.VMEM((2, 8, 128), f32),
            pltpu.VMEM((2, 2, 16, 128), f32),
            dma((3,)),
            dma((3,)), dma((3,)),
            dma((4,)), dma((4,)),
            dma((terms - 1,)), dma((terms,)),
            dma((terms,)), dma((terms,)),
            dma((terms,)), dma((terms,)),
            dma((ITERS, nx)), dma((ITERS, nx)),
            dma((3,)), dma((3,)),
        ],
        compiler_params=pltpu.CompilerParams(
            collective_id=0, has_side_effects=True, vmem_limit_bytes=63 * 2**20
        ),
    )(rhs, coef, env)
    def place(a_ref, b_ref, c_ref, d_ref):
        for i in range(strip):
            c_ref[:, i, :] = a_ref[i]
            d_ref[:, i, :] = b_ref[i]

    final = jax.ShapeDtypeStruct((rows, strip, ny), f32)
    return pl.pallas_call(
        place,
        out_shape=(final, final),
        in_specs=[pl.BlockSpec(memory_space=pltpu.VMEM)] * 2,
        out_specs=(pl.BlockSpec(memory_space=pltpu.VMEM),) * 2,
    )(sol, res)


def fits(mesh, rhs):
    cells = rhs.shape[1] * mesh.shape["grid"] * rhs.shape[2]
    return mesh.shape["rank"] == 4 and mesh.shape["grid"] == 2 and mesh.shape["term"] == 4 and rhs.shape[0] * 4 * cells * 4 <= 2**20


def solution(mesh):
    placed = (P("rank", "grid", None), P("term", "grid", None), P("term", "rank", None))

    def run(rhs, coef, env):
        if fits(mesh, rhs):
            return fused(mesh, rhs, coef, env)
        return shards(rhs, coef, env)

    return jax.shard_map(
        run,
        mesh=mesh,
        in_specs=placed,
        out_specs=(P("rank", "grid", None), P("rank", "grid", None)),
        check_vma=False,
    )
```

```python
import functools

import jax
import jax.numpy as jnp
from jax import lax
from jax.experimental import pallas as pl
from jax.experimental.pallas import tpu as pltpu
from jax.sharding import PartitionSpec as P

ITERS = 4
MESH = pl.DeviceIdType.MESH
CHUNK = 16


def padded_2(block, sides, width):
    for axis, dim in sides:
        count = lax.axis_size(axis)
        forward = [(i, i + 1) for i in range(count - 1)]
        backward = [(target, source) for source, target in forward]
        low = lax.ppermute(
            lax.slice_in_dim(block, block.shape[dim] - width, None, axis=dim), axis, forward
        )
        high = lax.ppermute(lax.slice_in_dim(block, 0, width, axis=dim), axis, backward)
        block = jnp.concatenate([low, block, high], axis=dim)
    return block


def face_weights(padded):
    wide = jnp.pad(padded, ((0, 0), (0, 0), (1, 1)))
    centre = wide[:, 1:-1, 1:-1]
    face_up = 0.5 * (centre + wide[:, 2:, 1:-1])
    face_down = 0.5 * (centre + wide[:, :-2, 1:-1])
    face_right = 0.5 * (centre + wide[:, 1:-1, 2:])
    face_left = 0.5 * (centre + wide[:, 1:-1, :-2])
    return (face_up + face_down + face_right + face_left, face_up, face_down, face_right, face_left)


def apply_faces(field, faces):
    middle = field[..., 1:-1, :]
    sideways = jnp.pad(middle, [(0, 0)] * (middle.ndim - 1) + [(1, 1)])
    total, face_up, face_down, face_right, face_left = faces
    return (
        total * middle
        - face_up * field[..., 2:, :]
        - face_down * field[..., :-2, :]
        - face_right * sideways[..., 2:]
        - face_left * sideways[..., :-2]
    )


def shards(rhs, coef, env):
    coef_padded = padded_2(coef, (("grid", 1),), 1)
    faces = tuple((weights[:, None] for weights in face_weights(coef_padded)))

    def square_sum(vector):
        return lax.psum(jnp.sum(vector * vector), ("grid", "rank"))

    solution = jnp.zeros(rhs.shape, jnp.float32)
    residual = rhs
    direction = rhs
    norm_now = square_sum(residual)
    for step in range(ITERS):
        padded = padded_2(direction, (("grid", 1),), 1)
        stenciled = apply_faces(padded[None], faces)
        image = lax.psum_scatter(
            jnp.einsum("krs,krxy->sxy", env, stenciled, precision=lax.Precision.HIGHEST),
            "rank",
            scatter_dimension=0,
            tiled=True,
        )
        image = lax.psum(image, "term")
        alpha = norm_now / lax.psum(jnp.sum(direction * image), ("grid", "rank"))
        solution = solution + alpha * direction
        residual = residual - alpha * image
        norm_next = square_sum(residual)
        direction = residual + norm_next / norm_now * direction
        norm_now = norm_next
    return (solution, residual)


def shift_sum(v):
    lane = lax.broadcasted_iota(jnp.int32, v.shape, v.ndim - 1)
    n = v.shape[-1]
    axis = v.ndim - 1
    left = jnp.where(lane == 0, 0.0, pltpu.roll(v, 1, axis))
    right = jnp.where(lane == n - 1, 0.0, pltpu.roll(v, n - 1, axis))
    return left + right


def neighbours(read, x, count):
    total = shift_sum(read(x))
    if x > 0:
        total = total + read(x - 1)
    if x < count - 1:
        total = total + read(x + 1)
    return total


def split3(v):
    high = v.astype(jnp.bfloat16)
    low = (v - high.astype(jnp.float32)).astype(jnp.bfloat16)
    return jnp.concatenate([high, high, low], axis=0)


def total_sum(v):
    return jnp.sum(v, axis=(0, 1), keepdims=True)


def cg_kernel(
    sizes,
    rhs_ref, coef_ref, env_ref,
    sol_ref, out_ref,
    rhs_own, env_all, coef_all, coef_tab, faces, stack, residual, image, keep, down, gathered, split_rhs, trace, gram,
    load, rhs_send, rhs_recv, sib_send, sib_recv, env_send, env_recv, envy_send, envy_recv,
    coef_send, coef_recv, img_send, img_recv, sum_send, sum_recv,
):
    terms, per, rows, strip, ny, ranks = sizes
    grids, ys = 2, 2
    nx = grids * strip
    half = ys * rows
    count = terms * per
    gx = lax.axis_index("grid")
    rank = lax.axis_index("rank")
    gz = lax.axis_index("term")
    gy = rank // 2
    core = rank % 2
    sibling = (gx, gy * 2 + (1 - core), gz)

    def at(x, y, z):
        return (x, y * 2 + core, z)

    origins = [gz + 1 - 2 * (gz % 2), 2 - gz // 2, 3 - 3 * (gz // 2)]
    over_x, over_y, across = at(1 - gx, gy, gz), at(gx, 1 - gy, gz), at(1 - gx, 1 - gy, gz)
    line = [at(gx, gy, o) for o in origins]

    barrier = pltpu.get_barrier_semaphore()

    def greet(peer):
        pl.semaphore_signal(barrier, inc=1, device_id=peer, device_id_type=MESH)

    peers = line[::-1] + [across, over_x, over_y, sibling]
    for peer in peers:
        greet(peer)

    loads = [
        pltpu.make_async_copy(rhs_ref, rhs_own, load.at[0]),
        pltpu.make_async_copy(env_ref, env_all.at[gz, :, gy], load.at[1]),
        pltpu.make_async_copy(coef_ref, coef_all.at[gz, gx], load.at[2]),
    ]
    for copy in loads:
        copy.start()

    loads[0].wait()
    for i in range(strip):
        residual[gx * strip + i, gy, core] = rhs_own[:, i, :]
    loads[1].wait()
    loads[2].wait()
    pl.semaphore_wait(barrier, len(peers))

    sent = []

    def remote(src, dst, send, recv, device):
        return pltpu.make_async_remote_copy(
            src_ref=src, dst_ref=dst, send_sem=send, recv_sem=recv, device_id=device, device_id_type=MESH
        )

    def push(block, send, recv, device):
        copy = remote(block, block, send, recv, device)
        sent.append(copy)
        copy.start()
        return copy

    def arrived(block, recv):
        remote(block, block, sib_send.at[0], recv, sibling).wait_recv()

    def strip_of(x, y):
        return residual.at[pl.ds(x * strip, strip), y, core]

    def env_line(o):
        return env_all.at[o, :, gy]

    own = strip_of(gx, gy)
    for i in (2, 1, 0):
        push(coef_all.at[gz, gx], coef_send.at[i], coef_recv.at[gz], line[i])
    for i in (2, 1, 0):
        push(env_line(gz), env_send.at[i], env_recv.at[gz], line[i])
    push(env_line(gz), envy_send.at[3], envy_recv.at[gz], over_y)
    rhs_y = push(own, rhs_send.at[0], rhs_recv.at[0], over_y)
    rhs_x = push(own, rhs_send.at[1], rhs_recv.at[1], over_x)
    rhs_d = push(own, rhs_send.at[2], rhs_recv.at[2], across)
    sibs = [push(own, sib_send.at[0], sib_recv.at[0], sibling)]

    def put_stack(o):
        for i in range(per):
            block = env_all[o, i].reshape(half, ranks)
            high = block.astype(jnp.bfloat16)
            low = (block - high.astype(jnp.float32)).astype(jnp.bfloat16)
            for c in range(half // CHUNK):
                at = pl.ds(pl.multiple_of(c * count * CHUNK + (o * per + i) * CHUNK, CHUNK), CHUNK)
                piece = slice(c * CHUNK, (c + 1) * CHUNK)
                stack[at, 0:ranks] = high[piece]
                stack[at, ranks : 2 * ranks] = low[piece]
                stack[at, 2 * ranks : 3 * ranks] = high[piece]

    def cross(i):
        o = origins[i]
        arrived(env_line(o), env_recv.at[o])
        push(env_line(o), envy_send.at[i], envy_recv.at[o], over_y)

    def to_sibling(i, copy, x, y):
        copy.wait_recv()
        sibs.append(push(strip_of(x, y), sib_send.at[i], sib_recv.at[i], sibling))

    def crossed_into_stack(o):
        arrived(env_all.at[o, :, 1 - gy], envy_recv.at[o])
        put_stack(o)

    for o in origins:
        arrived(coef_all.at[o, gx], coef_recv.at[o])
    coef_x = push(coef_all.at[:, gx], coef_send.at[terms - 1], coef_recv.at[gz], over_x)
    cross(0)
    to_sibling(1, rhs_y, gx, 1 - gy)
    to_sibling(2, rhs_x, 1 - gx, gy)
    cross(1)
    to_sibling(3, rhs_d, 1 - gx, 1 - gy)
    cross(2)
    coef_x.wait_recv()
    for x in range(nx):
        for i in range(per):
            coef_tab[x, :, i, :] = coef_all[:, x // strip, i, x % strip, :]
    for x in range(nx):
        here = coef_tab[x]
        lane = lax.broadcasted_iota(jnp.int32, here.shape, 2)
        after = jnp.where(lane == ny - 1, 0.0, pltpu.roll(here, ny - 1, 2))
        before = jnp.where(lane == 0, 0.0, pltpu.roll(here, 1, 2))
        faces[0, x] = 0.5 * (here + after)
        faces[1, x] = 0.5 * (here + before)
        faces[2, x] = 0.5 * (here + coef_tab[x - 1] if x > 0 else here)
        faces[3, x] = 0.5 * (here + coef_tab[x + 1] if x < nx - 1 else here)

    def image_copy(x, slot):
        block = image.at[slot, pl.ds(x, 2 if x == nx - 2 else 1), :, core]
        return remote(block, block, img_send.at[slot, x], img_recv.at[slot, x], sibling)

    per_y = rows // CHUNK

    def vector(t, x, y, span=slice(None)):
        ref = residual if t == 0 else image.at[t - 1]
        return ref[x, y, core, span, :]

    def emit(slot, x, c, value):
        span = slice((c % per_y) * CHUNK, (c % per_y + 1) * CHUNK)
        image[slot, x, c // per_y, core, span, :] = value * inverse - vector(slot, x, c // per_y, span)

    def weighted(block, x, pairs, sums):
        for n, (z, i) in enumerate(pairs):
            term = block[n * CHUNK : (n + 1) * CHUNK]
            for a in range(4):
                value = faces[a, x, z, i : i + 1, :] * term
                sums[a] = value if sums[a] is None else sums[a] + value

    def settle(x, c, slot, sums):
        lane = lax.broadcasted_iota(jnp.int32, sums[0].shape, 1)
        value = (sums[0] + sums[1]) + (sums[2] + sums[3])
        value = value - jnp.where(lane == 0, 0.0, pltpu.roll(sums[0], 1, 1))
        value = value - jnp.where(lane == ny - 1, 0.0, pltpu.roll(sums[1], ny - 1, 1))
        piece = slice(c * CHUNK, (c + 1) * CHUNK)
        if x > 0:
            value = value - down[x - 1, piece, :]
            emit(slot, x - 1, c, keep[x - 1, piece, :] - sums[2])
        if x < nx - 1:
            down[x, piece, :] = sums[3]
            keep[x, piece, :] = value
        else:
            emit(slot, x, c, value)

    def send_rows(x, slot):
        if slot < ITERS - 1 and x > 0 and x < nx - 1:
            image_copy(x - 1, slot).start()
        elif slot < ITERS - 1 and x == nx - 1:
            image_copy(nx - 2, slot).start()

    def product(x, field, slot):
        parts = split3(field)
        for c in range(half // CHUNK):
            span = slice(c * count * CHUNK, (c + 1) * count * CHUNK)
            block = jnp.dot(stack[span, :], parts, preferred_element_type=jnp.float32)
            sums = [None] * 4
            weighted(block, x, [(z, i) for z in range(terms) for i in range(per)], sums)
            settle(x, c, slot, sums)
        send_rows(x, slot)

    def first_product(o, begin, end):
        wide = per * CHUNK
        for x in range(nx):
            lines = [
                stack[pl.ds(pl.multiple_of((c * terms + o) * wide, CHUNK), wide), :]
                for c in range(half // CHUNK)
            ]
            block = jnp.dot(jnp.concatenate(lines, axis=0), split_rhs[x], preferred_element_type=jnp.float32)
            for c in range(half // CHUNK):
                piece = slice(c * CHUNK, (c + 1) * CHUNK)
                sums = [None] * 4
                if not begin:
                    for a in range(4):
                        sums[a] = gathered[a, x, piece, :]
                weighted(block[c * wide : (c + 1) * wide], x, [(o, i) for i in range(per)], sums)
                if end:
                    settle(x, c, 0, sums)
                else:
                    for a in range(4):
                        gathered[a, x, piece, :] = sums[a]
            if end:
                send_rows(x, 0)

    def folded(v):
        return jnp.sum(v.reshape(v.shape[0] // 8, 8, v.shape[1]), axis=0)

    def paired(block, send):
        return remote(block, block, sum_send.at[send], sum_recv.at[send], sibling)

    def diagonal():
        shape = (rows, ranks)
        row = lax.broadcasted_iota(jnp.int32, shape, 0)
        column = lax.broadcasted_iota(jnp.int32, shape, 1)
        on = column == row + rank * rows
        weight = sum(faces[a, x] for a in range(4) for x in range(nx))
        weight = jnp.sum(weight, axis=2, keepdims=True)
        total = jnp.zeros((8, ranks), jnp.float32)
        for z in range(terms):
            for i in range(per):
                entries = jnp.where(on, jnp.abs(env_all[z, i, gy]), 0.0)
                total = total + weight[z, i : i + 1, :] * folded(entries)
        return total

    def grams(part, pairs):
        sums = [None] * len(pairs)
        needed = sorted({t for pair in pairs for t in pair})
        for x in range(nx):
            for y in range(ys):
                fields = {t: vector(t, x, y) for t in needed}
                for n, (i, j) in enumerate(pairs):
                    value = folded(fields[i] * fields[j])
                    sums[n] = value if sums[n] is None else sums[n] + value
        for value, pair in zip(sums, pairs):
            line = jnp.sum(sum(value[:, l : l + 128] for l in range(0, ny, 128)), axis=0, keepdims=True)
            n = order[part].index(pair)
            gram[part, core, n : n + 1, :] = line

    def gram_copy(part):
        return paired(gram.at[part, core], part)

    def gram_sums(part):
        both = jnp.sum(gram[part, 0] + gram[part, 1], axis=1, keepdims=True)
        return {pair: both[n : n + 1, :] for n, pair in enumerate(order[part])}

    last = ITERS
    order = (
        [(i, j) for j in range(last) for i in range(j + 1)],
        [(i, last) for i in range(last)],
    )

    crossed_into_stack(gz)
    for copy in sibs:
        copy.wait_recv()
    for x in range(nx):
        split_rhs[x] = split3(residual[x].reshape(ranks, ny))
    trace[core] = diagonal()
    trace_copy = paired(trace.at[core], 2)
    trace_copy.start()
    gram[...] = jnp.zeros_like(gram)
    inverse = None
    first_product(gz, True, False)
    for i, o in enumerate(origins):
        crossed_into_stack(o)
        if i == len(origins) - 1:
            trace_copy.wait_recv()
            size = total_sum(trace[0] + trace[1]) * (1.0 / (half * nx * ny))
            theta = jnp.where(size > 0.0, size, 1.0)
            inverse = 1.0 / theta
        first_product(o, False, i == len(origins) - 1)
    grams(0, [(0, 0), (0, 1), (1, 1)])

    def mixed(left, right, table):
        total = None
        for i, a in enumerate(left):
            inner = None
            for j, b in enumerate(right):
                value = b * table[min(i, j), max(i, j)]
                inner = value if inner is None else inner + value
            total = a * inner if total is None else total + a * inner
        return total

    def applied(d):
        return [d[0]] + [d[j] + d[j - 1] for j in range(1, len(d))] + [d[-1]]

    def updated(sol, left, d, image_d, alpha):
        sol = [a + alpha * b for a, b in zip(sol, d)] + [alpha * b for b in d[len(sol) :]]
        left = [a - alpha * b for a, b in zip(left, image_d)] + [-alpha * image_d[-1]]
        return sol, left

    for step in range(1, ITERS):
        for x in range(nx):
            if x < nx - 1:
                image_copy(x, step - 1).wait_recv()
            if step == ITERS - 1 and x == nx - 1:
                gram_copy(0).wait_recv()
            product(x, image[step - 1, x].reshape(ranks, ny), step)
        if step < ITERS - 1:
            grams(0, [(i, step + 1) for i in range(step + 2)])
            if step == ITERS - 2:
                gram_copy(0).start()

    table = gram_sums(0)
    one = jnp.ones_like(theta)
    sol, left, d, norm = [], [one], [one], table[0, 0]
    for step in range(ITERS - 1):
        image_d = applied(d)
        alpha = norm / mixed(d, image_d, table)
        sol, left = updated(sol, left, d, image_d, alpha)
        fresh = mixed(left, left, table)
        beta = fresh / norm
        d = [a + beta * b for a, b in zip(left, d)] + [left[-1]]
        norm = fresh
    image_d = applied(d)
    known = mixed(d, image_d[:-1], table)

    grams(1, order[1])
    copy = gram_copy(1)
    copy.start()
    copy.wait_recv()
    rest = gram_sums(1)
    tail = sum(d[i] * rest[i, last] for i in range(last))
    alpha = norm / (known + image_d[-1] * tail)
    sol, left = updated(sol, left, d, image_d, alpha)
    sol = [a * inverse for a in sol]
    for i in range(strip):
        fields = [vector(t, gx * strip + i, gy) for t in range(ITERS + 1)]
        sol_ref[i] = sum(a * v for a, v in zip(sol, fields))
        out_ref[i] = sum(a * v for a, v in zip(left, fields))

    for slot in range(ITERS - 1):
        for x in range(nx - 1):
            image_copy(x, slot).wait_send()
    for copy in sent + [trace_copy, gram_copy(0), gram_copy(1)]:
        copy.wait_send()


def fused(mesh, rhs, coef, env):
    terms = mesh.shape["term"]
    rows, strip, ny = rhs.shape
    per, ranks = env.shape[0], env.shape[2]
    grids, ys = 2, 2
    nx, half, count = grids * strip, ys * rows, per * terms
    sizes = (terms, per, rows, strip, ny, ranks)
    f32 = jnp.float32
    dma = pltpu.SemaphoreType.DMA
    block = jax.ShapeDtypeStruct((strip, rows, ny), f32)
    sol, res = pl.pallas_call(
        functools.partial(cg_kernel, sizes),
        out_shape=(block, block),
        in_specs=[pl.BlockSpec(memory_space=pltpu.HBM)] * 3,
        out_specs=(pl.BlockSpec(memory_space=pltpu.VMEM),) * 2,
        scratch_shapes=[
            pltpu.VMEM((rows, strip, ny), f32),
            pltpu.VMEM((terms, per, ys, rows, ranks), f32),
            pltpu.VMEM((terms, grids, per, strip, ny), f32),
            pltpu.VMEM((nx, terms, per, ny), f32),
            pltpu.VMEM((4, nx, terms, per, ny), f32),
            pltpu.VMEM((count * half, 3 * ranks), jnp.bfloat16),
            pltpu.VMEM((nx, ys, 2, rows, ny), f32),
            pltpu.VMEM((ITERS, nx, ys, 2, rows, ny), f32),
            pltpu.VMEM((nx, half, ny), f32),
            pltpu.VMEM((nx, half, ny), f32),
            pltpu.VMEM((4, nx, half, ny), f32),
            pltpu.VMEM((nx, 3 * ranks, ny), jnp.bfloat16),
            pltpu.VMEM((2, 8, 128), f32),
            pltpu.VMEM((2, 2, 16, 128), f32),
            dma((3,)),
            dma((3,)), dma((3,)),
            dma((4,)), dma((4,)),
            dma((terms - 1,)), dma((terms,)),
            dma((terms,)), dma((terms,)),
            dma((terms,)), dma((terms,)),
            dma((ITERS, nx)), dma((ITERS, nx)),
            dma((3,)), dma((3,)),
        ],
        compiler_params=pltpu.CompilerParams(
            collective_id=0, has_side_effects=True, vmem_limit_bytes=63 * 2**20
        ),
    )(rhs, coef, env)
    def place(a_ref, b_ref, c_ref, d_ref):
        for i in range(strip):
            c_ref[:, i, :] = a_ref[i]
            d_ref[:, i, :] = b_ref[i]

    final = jax.ShapeDtypeStruct((rows, strip, ny), f32)
    return pl.pallas_call(
        place,
        out_shape=(final, final),
        in_specs=[pl.BlockSpec(memory_space=pltpu.VMEM)] * 2,
        out_specs=(pl.BlockSpec(memory_space=pltpu.VMEM),) * 2,
    )(sol, res)


def fits(mesh, rhs):
    cells = rhs.shape[1] * mesh.shape["grid"] * rhs.shape[2]
    return mesh.shape["rank"] == 4 and mesh.shape["grid"] == 2 and mesh.shape["term"] == 4 and rhs.shape[0] * 4 * cells * 4 <= 2**20


def solution(mesh):
    placed = (P("rank", "grid", None), P("term", "grid", None), P("term", "rank", None))

    def run(rhs, coef, env):
        if fits(mesh, rhs):
            return fused(mesh, rhs, coef, env)
        return shards(rhs, coef, env)

    return jax.shard_map(
        run,
        mesh=mesh,
        in_specs=placed,
        out_specs=(P("rank", "grid", None), P("rank", "grid", None)),
        check_vma=False,
    )
```

```python
import functools

import jax
import jax.numpy as jnp
from jax import lax
from jax.experimental import pallas as pl
from jax.experimental.pallas import tpu as pltpu
from jax.sharding import PartitionSpec as P

ITERS = 4
MESH = pl.DeviceIdType.MESH
CHUNK = 16


def padded_2(block, sides, width):
    for axis, dim in sides:
        count = lax.axis_size(axis)
        forward = [(i, i + 1) for i in range(count - 1)]
        backward = [(target, source) for source, target in forward]
        low = lax.ppermute(
            lax.slice_in_dim(block, block.shape[dim] - width, None, axis=dim), axis, forward
        )
        high = lax.ppermute(lax.slice_in_dim(block, 0, width, axis=dim), axis, backward)
        block = jnp.concatenate([low, block, high], axis=dim)
    return block


def face_weights(padded):
    wide = jnp.pad(padded, ((0, 0), (0, 0), (1, 1)))
    centre = wide[:, 1:-1, 1:-1]
    face_up = 0.5 * (centre + wide[:, 2:, 1:-1])
    face_down = 0.5 * (centre + wide[:, :-2, 1:-1])
    face_right = 0.5 * (centre + wide[:, 1:-1, 2:])
    face_left = 0.5 * (centre + wide[:, 1:-1, :-2])
    return (face_up + face_down + face_right + face_left, face_up, face_down, face_right, face_left)


def apply_faces(field, faces):
    middle = field[..., 1:-1, :]
    sideways = jnp.pad(middle, [(0, 0)] * (middle.ndim - 1) + [(1, 1)])
    total, face_up, face_down, face_right, face_left = faces
    return (
        total * middle
        - face_up * field[..., 2:, :]
        - face_down * field[..., :-2, :]
        - face_right * sideways[..., 2:]
        - face_left * sideways[..., :-2]
    )


def shards(rhs, coef, env):
    coef_padded = padded_2(coef, (("grid", 1),), 1)
    faces = tuple((weights[:, None] for weights in face_weights(coef_padded)))

    def square_sum(vector):
        return lax.psum(jnp.sum(vector * vector), ("grid", "rank"))

    solution = jnp.zeros(rhs.shape, jnp.float32)
    residual = rhs
    direction = rhs
    norm_now = square_sum(residual)
    for step in range(ITERS):
        padded = padded_2(direction, (("grid", 1),), 1)
        stenciled = apply_faces(padded[None], faces)
        image = lax.psum_scatter(
            jnp.einsum("krs,krxy->sxy", env, stenciled, precision=lax.Precision.HIGHEST),
            "rank",
            scatter_dimension=0,
            tiled=True,
        )
        image = lax.psum(image, "term")
        alpha = norm_now / lax.psum(jnp.sum(direction * image), ("grid", "rank"))
        solution = solution + alpha * direction
        residual = residual - alpha * image
        norm_next = square_sum(residual)
        direction = residual + norm_next / norm_now * direction
        norm_now = norm_next
    return (solution, residual)


def shift_sum(v):
    lane = lax.broadcasted_iota(jnp.int32, v.shape, v.ndim - 1)
    n = v.shape[-1]
    axis = v.ndim - 1
    left = jnp.where(lane == 0, 0.0, pltpu.roll(v, 1, axis))
    right = jnp.where(lane == n - 1, 0.0, pltpu.roll(v, n - 1, axis))
    return left + right


def neighbours(read, x, count):
    total = shift_sum(read(x))
    if x > 0:
        total = total + read(x - 1)
    if x < count - 1:
        total = total + read(x + 1)
    return total


def split3(v):
    high = v.astype(jnp.bfloat16)
    low = (v - high.astype(jnp.float32)).astype(jnp.bfloat16)
    return jnp.concatenate([high, high, low], axis=0)


def total_sum(v):
    return jnp.sum(v, axis=(0, 1), keepdims=True)


def cg_kernel(
    sizes,
    rhs_ref, coef_ref, env_ref,
    sol_ref, out_ref,
    rhs_own, env_all, coef_all, coef_tab, faces, stack, residual, image, keep, down, gathered, split_rhs, trace, gram,
    load, rhs_send, rhs_recv, sib_send, sib_recv, env_send, env_recv, envy_send, envy_recv,
    coef_send, coef_recv, img_send, img_recv, sum_send, sum_recv,
):
    terms, per, rows, strip, ny, ranks = sizes
    grids, ys = 2, 2
    nx = grids * strip
    half = ys * rows
    count = terms * per
    gx = lax.axis_index("grid")
    rank = lax.axis_index("rank")
    gz = lax.axis_index("term")
    gy = rank // 2
    core = rank % 2
    sibling = (gx, gy * 2 + (1 - core), gz)

    def at(x, y, z):
        return (x, y * 2 + core, z)

    origins = [gz + 1 - 2 * (gz % 2), 2 - gz // 2, 3 - 3 * (gz // 2)]
    over_x, over_y, across = at(1 - gx, gy, gz), at(gx, 1 - gy, gz), at(1 - gx, 1 - gy, gz)
    line = [at(gx, gy, o) for o in origins]

    barrier = pltpu.get_barrier_semaphore()

    def greet(peer):
        pl.semaphore_signal(barrier, inc=1, device_id=peer, device_id_type=MESH)

    peers = line[::-1] + [across, over_x, over_y, sibling]
    for peer in peers:
        greet(peer)

    loads = [
        pltpu.make_async_copy(rhs_ref, rhs_own, load.at[0]),
        pltpu.make_async_copy(env_ref, env_all.at[gz, :, gy], load.at[1]),
        pltpu.make_async_copy(coef_ref, coef_all.at[gz, gx], load.at[2]),
    ]
    for copy in loads:
        copy.start()

    loads[0].wait()
    for i in range(strip):
        residual[gx * strip + i, gy, core] = rhs_own[:, i, :]
    loads[1].wait()
    loads[2].wait()
    pl.semaphore_wait(barrier, len(peers))

    sent = []

    def remote(src, dst, send, recv, device):
        return pltpu.make_async_remote_copy(
            src_ref=src, dst_ref=dst, send_sem=send, recv_sem=recv, device_id=device, device_id_type=MESH
        )

    def push(block, send, recv, device):
        copy = remote(block, block, send, recv, device)
        sent.append(copy)
        copy.start()
        return copy

    def arrived(block, recv):
        remote(block, block, sib_send.at[0], recv, sibling).wait_recv()

    def strip_of(x, y):
        return residual.at[pl.ds(x * strip, strip), y, core]

    def env_line(o):
        return env_all.at[o, :, gy]

    own = strip_of(gx, gy)
    sibs = [push(own, sib_send.at[0], sib_recv.at[0], sibling)]
    for i in (2, 1, 0):
        push(coef_all.at[gz, gx], coef_send.at[i], coef_recv.at[gz], line[i])
    for i in (2, 1, 0):
        push(env_line(gz), env_send.at[i], env_recv.at[gz], line[i])
    push(env_line(gz), envy_send.at[3], envy_recv.at[gz], over_y)
    rhs_y = push(own, rhs_send.at[0], rhs_recv.at[0], over_y)
    rhs_x = push(own, rhs_send.at[1], rhs_recv.at[1], over_x)
    rhs_d = push(own, rhs_send.at[2], rhs_recv.at[2], across)

    def put_stack(o):
        for i in range(per):
            block = env_all[o, i].reshape(half, ranks)
            high = block.astype(jnp.bfloat16)
            low = (block - high.astype(jnp.float32)).astype(jnp.bfloat16)
            for c in range(half // CHUNK):
                at = pl.ds(pl.multiple_of(c * count * CHUNK + (o * per + i) * CHUNK, CHUNK), CHUNK)
                piece = slice(c * CHUNK, (c + 1) * CHUNK)
                stack[at, 0:ranks] = high[piece]
                stack[at, ranks : 2 * ranks] = low[piece]
                stack[at, 2 * ranks : 3 * ranks] = high[piece]

    def cross(i):
        o = origins[i]
        arrived(env_line(o), env_recv.at[o])
        push(env_line(o), envy_send.at[i], envy_recv.at[o], over_y)

    def to_sibling(i, copy, x, y):
        copy.wait_recv()
        sibs.append(push(strip_of(x, y), sib_send.at[i], sib_recv.at[i], sibling))

    def crossed_into_stack(o):
        arrived(env_all.at[o, :, 1 - gy], envy_recv.at[o])
        put_stack(o)

    for o in origins:
        arrived(coef_all.at[o, gx], coef_recv.at[o])
    coef_x = push(coef_all.at[:, gx], coef_send.at[terms - 1], coef_recv.at[gz], over_x)
    cross(0)
    to_sibling(1, rhs_y, gx, 1 - gy)
    to_sibling(2, rhs_x, 1 - gx, gy)
    cross(1)
    to_sibling(3, rhs_d, 1 - gx, 1 - gy)
    cross(2)
    coef_x.wait_recv()
    for x in range(nx):
        for i in range(per):
            coef_tab[x, :, i, :] = coef_all[:, x // strip, i, x % strip, :]
    for x in range(nx):
        here = coef_tab[x]
        lane = lax.broadcasted_iota(jnp.int32, here.shape, 2)
        after = jnp.where(lane == ny - 1, 0.0, pltpu.roll(here, ny - 1, 2))
        before = jnp.where(lane == 0, 0.0, pltpu.roll(here, 1, 2))
        faces[0, x] = 0.5 * (here + after)
        faces[1, x] = 0.5 * (here + before)
        faces[2, x] = 0.5 * (here + coef_tab[x - 1] if x > 0 else here)
        faces[3, x] = 0.5 * (here + coef_tab[x + 1] if x < nx - 1 else here)

    def image_copy(x, slot):
        block = image.at[slot, pl.ds(x, 2 if x == nx - 2 else 1), :, core]
        return remote(block, block, img_send.at[slot, x], img_recv.at[slot, x], sibling)

    per_y = rows // CHUNK

    def vector(t, x, y, span=slice(None)):
        ref = residual if t == 0 else image.at[t - 1]
        return ref[x, y, core, span, :]

    def emit(slot, x, c, value):
        span = slice((c % per_y) * CHUNK, (c % per_y + 1) * CHUNK)
        image[slot, x, c // per_y, core, span, :] = value * inverse - vector(slot, x, c // per_y, span)

    def weighted(block, x, pairs, sums):
        for n, (z, i) in enumerate(pairs):
            term = block[n * CHUNK : (n + 1) * CHUNK]
            for a in range(4):
                value = faces[a, x, z, i : i + 1, :] * term
                sums[a] = value if sums[a] is None else sums[a] + value

    def settle(x, c, slot, sums):
        lane = lax.broadcasted_iota(jnp.int32, sums[0].shape, 1)
        value = (sums[0] + sums[1]) + (sums[2] + sums[3])
        value = value - jnp.where(lane == 0, 0.0, pltpu.roll(sums[0], 1, 1))
        value = value - jnp.where(lane == ny - 1, 0.0, pltpu.roll(sums[1], ny - 1, 1))
        piece = slice(c * CHUNK, (c + 1) * CHUNK)
        if x > 0:
            value = value - down[x - 1, piece, :]
            emit(slot, x - 1, c, keep[x - 1, piece, :] - sums[2])
        if x < nx - 1:
            down[x, piece, :] = sums[3]
            keep[x, piece, :] = value
        else:
            emit(slot, x, c, value)

    def send_rows(x, slot):
        if slot < ITERS - 1 and x > 0 and x < nx - 1:
            image_copy(x - 1, slot).start()
        elif slot < ITERS - 1 and x == nx - 1:
            image_copy(nx - 2, slot).start()

    def product(x, field, slot):
        parts = split3(field)
        for c in range(half // CHUNK):
            span = slice(c * count * CHUNK, (c + 1) * count * CHUNK)
            block = jnp.dot(stack[span, :], parts, preferred_element_type=jnp.float32)
            sums = [None] * 4
            weighted(block, x, [(z, i) for z in range(terms) for i in range(per)], sums)
            settle(x, c, slot, sums)
        send_rows(x, slot)

    def first_product(o, begin, end):
        wide = per * CHUNK
        for x in range(nx):
            lines = [
                stack[pl.ds(pl.multiple_of((c * terms + o) * wide, CHUNK), wide), :]
                for c in range(half // CHUNK)
            ]
            block = jnp.dot(jnp.concatenate(lines, axis=0), split_rhs[x], preferred_element_type=jnp.float32)
            for c in range(half // CHUNK):
                piece = slice(c * CHUNK, (c + 1) * CHUNK)
                sums = [None] * 4
                if not begin:
                    for a in range(4):
                        sums[a] = gathered[a, x, piece, :]
                weighted(block[c * wide : (c + 1) * wide], x, [(o, i) for i in range(per)], sums)
                if end:
                    settle(x, c, 0, sums)
                else:
                    for a in range(4):
                        gathered[a, x, piece, :] = sums[a]
            if end:
                send_rows(x, 0)

    def folded(v):
        return jnp.sum(v.reshape(v.shape[0] // 8, 8, v.shape[1]), axis=0)

    def paired(block, send):
        return remote(block, block, sum_send.at[send], sum_recv.at[send], sibling)

    def diagonal():
        shape = (rows, ranks)
        row = lax.broadcasted_iota(jnp.int32, shape, 0)
        column = lax.broadcasted_iota(jnp.int32, shape, 1)
        on = column == row + rank * rows
        weight = sum(faces[a, x] for a in range(4) for x in range(nx))
        weight = jnp.sum(weight, axis=2, keepdims=True)
        total = jnp.zeros((8, ranks), jnp.float32)
        for z in range(terms):
            for i in range(per):
                entries = jnp.where(on, jnp.abs(env_all[z, i, gy]), 0.0)
                total = total + weight[z, i : i + 1, :] * folded(entries)
        return total

    def grams(part, pairs):
        sums = [None] * len(pairs)
        needed = sorted({t for pair in pairs for t in pair})
        for x in range(nx):
            for y in range(ys):
                fields = {t: vector(t, x, y) for t in needed}
                for n, (i, j) in enumerate(pairs):
                    value = folded(fields[i] * fields[j])
                    sums[n] = value if sums[n] is None else sums[n] + value
        for value, pair in zip(sums, pairs):
            line = jnp.sum(sum(value[:, l : l + 128] for l in range(0, ny, 128)), axis=0, keepdims=True)
            n = order[part].index(pair)
            gram[part, core, n : n + 1, :] = line

    def gram_copy(part):
        return paired(gram.at[part, core], part)

    def gram_sums(part):
        both = jnp.sum(gram[part, 0] + gram[part, 1], axis=1, keepdims=True)
        return {pair: both[n : n + 1, :] for n, pair in enumerate(order[part])}

    last = ITERS
    order = (
        [(i, j) for j in range(last) for i in range(j + 1)],
        [(i, last) for i in range(last)],
    )

    crossed_into_stack(gz)
    for copy in sibs:
        copy.wait_recv()
    for x in range(nx):
        split_rhs[x] = split3(residual[x].reshape(ranks, ny))
    trace[core] = diagonal()
    trace_copy = paired(trace.at[core], 2)
    trace_copy.start()
    gram[...] = jnp.zeros_like(gram)
    inverse = None
    first_product(gz, True, False)
    for i, o in enumerate(origins):
        crossed_into_stack(o)
        if i == len(origins) - 1:
            trace_copy.wait_recv()
            size = total_sum(trace[0] + trace[1]) * (1.0 / (half * nx * ny))
            theta = jnp.where(size > 0.0, size, 1.0)
            inverse = 1.0 / theta
        first_product(o, False, i == len(origins) - 1)
    grams(0, [(0, 0), (0, 1), (1, 1)])
    for copy in sent + [trace_copy]:
        copy.wait_send()

    def mixed(left, right, table):
        total = None
        for i, a in enumerate(left):
            inner = None
            for j, b in enumerate(right):
                value = b * table[min(i, j), max(i, j)]
                inner = value if inner is None else inner + value
            total = a * inner if total is None else total + a * inner
        return total

    def applied(d):
        return [d[0]] + [d[j] + d[j - 1] for j in range(1, len(d))] + [d[-1]]

    def updated(sol, left, d, image_d, alpha):
        sol = [a + alpha * b for a, b in zip(sol, d)] + [alpha * b for b in d[len(sol) :]]
        left = [a - alpha * b for a, b in zip(left, image_d)] + [-alpha * image_d[-1]]
        return sol, left

    for step in range(1, ITERS):
        for x in range(nx):
            if x < nx - 1:
                image_copy(x, step - 1).wait_recv()
            if step == ITERS - 1 and x == nx - 1:
                gram_copy(0).wait_recv()
            product(x, image[step - 1, x].reshape(ranks, ny), step)
        if step < ITERS - 1:
            grams(0, [(i, step + 1) for i in range(step + 2)])
            if step == ITERS - 2:
                gram_copy(0).start()
            for x in range(nx - 1):
                image_copy(x, step - 1).wait_send()

    grams(1, order[1])
    copy = gram_copy(1)
    copy.start()
    table = gram_sums(0)
    one = jnp.ones_like(theta)
    sol, left, d, norm = [], [one], [one], table[0, 0]
    for step in range(ITERS - 1):
        image_d = applied(d)
        alpha = norm / mixed(d, image_d, table)
        sol, left = updated(sol, left, d, image_d, alpha)
        fresh = mixed(left, left, table)
        beta = fresh / norm
        d = [a + beta * b for a, b in zip(left, d)] + [left[-1]]
        norm = fresh
    image_d = applied(d)
    known = mixed(d, image_d[:-1], table)
    mine = []
    for i in range(strip):
        fields = [vector(t, gx * strip + i, gy) for t in range(ITERS + 1)]
        mine.append([sum(a * v for a, v in zip(line, fields)) for line in (sol, d, left, image_d)])
    for x in range(nx - 1):
        image_copy(x, ITERS - 2).wait_send()
    gram_copy(0).wait_send()
    copy.wait()
    rest = gram_sums(1)
    tail = sum(d[i] * rest[i, last] for i in range(last))
    alpha = norm / (known + image_d[-1] * tail)
    for i, (found, way, rest_left, image_way) in enumerate(mine):
        sol_ref[i] = (found + alpha * way) * inverse
        out_ref[i] = rest_left - alpha * image_way


def fused(mesh, rhs, coef, env):
    terms = mesh.shape["term"]
    rows, strip, ny = rhs.shape
    per, ranks = env.shape[0], env.shape[2]
    grids, ys = 2, 2
    nx, half, count = grids * strip, ys * rows, per * terms
    sizes = (terms, per, rows, strip, ny, ranks)
    f32 = jnp.float32
    dma = pltpu.SemaphoreType.DMA
    block = jax.ShapeDtypeStruct((strip, rows, ny), f32)
    sol, res = pl.pallas_call(
        functools.partial(cg_kernel, sizes),
        out_shape=(block, block),
        in_specs=[pl.BlockSpec(memory_space=pltpu.HBM)] * 3,
        out_specs=(pl.BlockSpec(memory_space=pltpu.VMEM),) * 2,
        scratch_shapes=[
            pltpu.VMEM((rows, strip, ny), f32),
            pltpu.VMEM((terms, per, ys, rows, ranks), f32),
            pltpu.VMEM((terms, grids, per, strip, ny), f32),
            pltpu.VMEM((nx, terms, per, ny), f32),
            pltpu.VMEM((4, nx, terms, per, ny), f32),
            pltpu.VMEM((count * half, 3 * ranks), jnp.bfloat16),
            pltpu.VMEM((nx, ys, 2, rows, ny), f32),
            pltpu.VMEM((ITERS, nx, ys, 2, rows, ny), f32),
            pltpu.VMEM((nx, half, ny), f32),
            pltpu.VMEM((nx, half, ny), f32),
            pltpu.VMEM((4, nx, half, ny), f32),
            pltpu.VMEM((nx, 3 * ranks, ny), jnp.bfloat16),
            pltpu.VMEM((2, 8, 128), f32),
            pltpu.VMEM((2, 2, 16, 128), f32),
            dma((3,)),
            dma((3,)), dma((3,)),
            dma((4,)), dma((4,)),
            dma((terms - 1,)), dma((terms,)),
            dma((terms,)), dma((terms,)),
            dma((terms,)), dma((terms,)),
            dma((ITERS, nx)), dma((ITERS, nx)),
            dma((3,)), dma((3,)),
        ],
        compiler_params=pltpu.CompilerParams(
            collective_id=0, has_side_effects=True, vmem_limit_bytes=63 * 2**20
        ),
    )(rhs, coef, env)
    def place(a_ref, b_ref, c_ref, d_ref):
        for i in range(strip):
            c_ref[:, i, :] = a_ref[i]
            d_ref[:, i, :] = b_ref[i]

    final = jax.ShapeDtypeStruct((rows, strip, ny), f32)
    return pl.pallas_call(
        place,
        out_shape=(final, final),
        in_specs=[pl.BlockSpec(memory_space=pltpu.VMEM)] * 2,
        out_specs=(pl.BlockSpec(memory_space=pltpu.VMEM),) * 2,
    )(sol, res)


def fits(mesh, rhs):
    cells = rhs.shape[1] * mesh.shape["grid"] * rhs.shape[2]
    return mesh.shape["rank"] == 4 and mesh.shape["grid"] == 2 and mesh.shape["term"] == 4 and rhs.shape[0] * 4 * cells * 4 <= 2**20


def solution(mesh):
    placed = (P("rank", "grid", None), P("term", "grid", None), P("term", "rank", None))

    def run(rhs, coef, env):
        if fits(mesh, rhs):
            return fused(mesh, rhs, coef, env)
        return shards(rhs, coef, env)

    return jax.shard_map(
        run,
        mesh=mesh,
        in_specs=placed,
        out_specs=(P("rank", "grid", None), P("rank", "grid", None)),
        check_vma=False,
    )
```
